32 devices in a mesh: dp: 16 (over z, y, x), seq: 2 (over core).
Axes of the slice: x: 2, y: 2, z: 4, core: 2. Of those that a mesh axis runs over, the one named last changes fastest.
Arguments:
- hidden_in: bfloat16 [16, 512, 768], P('dp', 'seq'), may hold values from -6 to 6
- w_qkv: bfloat16 [768, 2304], replicated, may hold values from -0.21875 to 0.21875
- b_qv: bfloat16 [2, 768], replicated, may hold values from -3 to 3
- w_o: bfloat16 [768, 768], replicated, may hold values from -2.5 to 2.5
- b_o: bfloat16 [768], replicated, may hold values from -3 to 3
- ln1_gain: bfloat16 [768], replicated, may hold values from 0.099609375 to 1.8984375
- ln1_bias: bfloat16 [768], replicated, may hold values from -3 to 3
- w_in: bfloat16 [768, 3072], replicated, may hold values from -0.21875 to 0.21875
- b_in: bfloat16 [3072], replicated, may hold values from -3 to 3
- w_out: bfloat16 [3072, 768], replicated, may hold values from -0.109375 to 0.109375
- b_out: bfloat16 [768], replicated, may hold values from -3 to 3
- ln2_gain: bfloat16 [768], replicated, may hold values from 0.099609375 to 1.8984375
- ln2_bias: bfloat16 [768], replicated, may hold values from -3 to 3
- seg_lengths: int32 [16, 4], P('dp'), may hold values from 1 to 509, as said below
- cotangent: bfloat16 [16, 512, 768], P('dp', 'seq'), may hold values from -6 to 6
Outputs:
- output: bfloat16 [16, 512, 768], P('dp', 'seq')
- pooled: float32 [16, 4, 768], P('dp')
- d_input: float32 [16, 512, 768], P('dp', 'seq')
- d_w_qkv: float32 [1769472], P(('dp', 'seq'))
- d_w_o: float32 [589824], P(('dp', 'seq'))
- d_w_in: float32 [2359296], P(('dp', 'seq'))
- d_w_out: float32 [2359296], P(('dp', 'seq'))
- d_b_qv: float32 [2, 768], replicated
- d_b_o: float32 [768], replicated
- d_ln1_gain: float32 [768], replicated
- d_ln1_bias: float32 [768], replicated
- d_b_in: float32 [3072], replicated
- d_b_out: float32 [768], replicated
- d_ln2_gain: float32 [768], replicated
- d_ln2_bias: float32 [768], replicated
The draws below stay inside these ranges and needn't reach their ends.
Inputs may be any that keep to these rules, and one draw needn't show every extreme that they name: `seg_lengths`: each row's 4 lengths add up to 512; no text ends at position 255, so some text of every row covers positions 255 and 256.
All inputs are finite; a program needn't handle non-finite values.
Results may differ from the reference program's by a relative error of at most 0.012.
Values may be sent and summed in bfloat16 or wider, within the bound.
No kernel may reach another device: no remote copies, remote signals or barrier semaphores. Data moves between devices by JAX's collectives and lax.ppermute only.
A program may use at most 192 MiB of HBM per device.

```python
import math
import jax
import jax.numpy as jnp
from jax import lax

D = 768
HEADS = 12
HEAD = 64
FF = 3072
LEN = 512
SEGS = 4
HALF = 256
ROWS = 16


def draw_seg_lengths(key, part):
    key = jax.random.fold_in(key, 7)
    offsets = jnp.arange(LEN - 2, dtype=jnp.int32) + 1
    candidates = offsets + (offsets >= HALF).astype(jnp.int32)

    def one_row(row_key):
        picked = jax.random.permutation(row_key, candidates)[:SEGS - 1]
        cut_points = jnp.sort(picked)
        end_points = jnp.concatenate([cut_points, jnp.full((1,), LEN, jnp.int32)])
        start_points = jnp.concatenate([jnp.zeros((1,), jnp.int32), cut_points])
        return end_points - start_points
    row_keys = jax.random.split(key, ROWS + 1)
    drawn = jax.vmap(one_row)(row_keys[1:])
    widest = jnp.concatenate([jnp.full((1,), LEN - SEGS + 1, jnp.int32), jnp.ones((SEGS - 1,), jnp.int32)])
    chosen = jax.random.randint(row_keys[0], (), 0, ROWS)
    row_index = jnp.arange(ROWS, dtype=jnp.int32)
    return jnp.where((row_index == chosen)[:, None], widest[None, :], drawn)


def block_scale(rng, extent, pieces, least, largest):
    def one(dim, parts):
        heights = jax.random.uniform(jax.random.fold_in(jax.random.fold_in(rng, 6), dim), (parts,), jnp.float32, least / len(pieces), largest / len(pieces))
        return jnp.repeat(jnp.exp(heights), extent[dim] // parts).reshape((-1,) + (1,) * (len(extent) - dim - 1))

    factor_of = one(*pieces[0])
    for cut in pieces[1:]:
        factor_of = factor_of * one(*cut)
    return factor_of


def normal_values(own_key, shape, scale, reach, shards=(), held_as=jnp.bfloat16):
    gain = block_scale(own_key, shape, shards, -0.22, 0.18) if shards else 1.0
    values = jax.random.normal(own_key, shape, jnp.float32) * scale * gain
    return jnp.minimum(jnp.maximum(values, -reach), reach).astype(held_as)


def setup_inputs(seed: int = 0) -> dict:
    key_list = jax.random.split(jax.random.key(seed), 16)
    hidden_in = normal_values(key_list[0], (ROWS, LEN, D), 1.0, 6.0, ((0, 16), (1, 2)))
    w_qkv = normal_values(key_list[1], (D, 3 * D), D ** -0.5, 0.21875)
    b_qv = normal_values(key_list[2], (2, D), 0.5, 3.0)
    w_o = normal_values(key_list[3], (D, D), (D * SEGS // LEN) ** -0.5, 2.5)
    b_o = normal_values(key_list[4], (D,), 0.5, 3.0)
    ln1_gain = jnp.clip(1.0 + 0.18 * jax.random.normal(key_list[5], (D,), jnp.float32), 0.099609375, 1.8984375).astype(jnp.bfloat16)
    ln1_bias = normal_values(key_list[6], (D,), 0.5, 3.0)
    w_in = normal_values(key_list[7], (D, FF), D ** -0.5, 0.21875)
    b_in = normal_values(key_list[8], (FF,), 0.5, 3.0)
    w_out = normal_values(key_list[9], (FF, D), FF ** -0.5, 0.109375)
    b_out = normal_values(key_list[10], (D,), 0.5, 3.0)
    ln2_gain = jnp.clip(1.0 + 0.18 * jax.random.normal(key_list[11], (D,), jnp.float32), 0.099609375, 1.8984375).astype(jnp.bfloat16)
    ln2_bias = normal_values(key_list[12], (D,), 0.5, 3.0)
    seg_lengths = draw_seg_lengths(jax.random.fold_in(key_list[15], 71), 0)
    cotangent = normal_values(key_list[14], (ROWS, LEN, D), 1.0, 6.0, ((0, 16), (1, 2)))
    return dict(hidden_in=hidden_in, w_qkv=w_qkv, b_qv=b_qv, w_o=w_o, b_o=b_o, ln1_gain=ln1_gain, ln1_bias=ln1_bias, w_in=w_in, b_in=b_in, w_out=w_out, b_out=b_out, ln2_gain=ln2_gain, ln2_bias=ln2_bias, seg_lengths=seg_lengths, cotangent=cotangent)


@jax.custom_vjp
def low(v):
    return lax.optimization_barrier(v.astype(jnp.bfloat16)).astype(jnp.float32)

@jax.custom_vjp
def low_back(v):
    return v

def low_keep(v):
    return (low(v), None)

def low_pass(kept, grad):
    return (grad,)

def back_keep(v):
    return (v, None)

def back_low(kept, grad):
    return (low(grad),)
low.defvjp(low_keep, low_pass)
low_back.defvjp(back_keep, back_low)
EPSILON = 1e-12

def matmul_high(left, right):
    return jnp.dot(left, right, precision=lax.Precision.HIGHEST)

def layer_norm(total, gain_vec, shift_vec):
    centered = total - lax.optimization_barrier(jnp.mean(total, axis=-1, keepdims=True))
    inverse = lax.rsqrt(lax.optimization_barrier(jnp.mean(centered * centered, axis=-1, keepdims=True)) + EPSILON)
    return centered * inverse * gain_vec + shift_vec

def segment_ids(lengths_in, positions):
    end_points = jnp.cumsum(lengths_in, axis=-1, dtype=jnp.int32)
    return lax.optimization_barrier(jnp.sum((positions[None, :, None] >= end_points[:, None, :]).astype(jnp.int32), axis=-1))

def forward(inputs, w_qkv, b_qv, w_o, b_o, ln1_gain, ln1_bias, w_in, b_in, w_out, b_out, ln2_gain, ln2_bias, same_seg):
    row_count = inputs.shape[0]
    flat_in = inputs.reshape(-1, D)
    qkv_lin = matmul_high(flat_in, w_qkv)
    queries = low_back(low(qkv_lin[:, :D] + b_qv[0]))
    keys_all = low_back(low(qkv_lin[:, D:2 * D]))
    values = low_back(low(qkv_lin[:, 2 * D:] + b_qv[1]))
    shaped = (row_count, LEN, HEADS, HEAD)
    raw = low_back(jnp.einsum('rphe,rqhe->rhpq', queries.reshape(shaped), keys_all.reshape(shaped), precision=lax.Precision.HIGHEST))
    scores = jnp.where(same_seg[:, None], raw * (1.0 / math.sqrt(HEAD)), -1e+30)
    probs_low = low(jax.nn.softmax(scores, axis=-1))
    attended = jnp.einsum('rhpq,rqhe->rphe', probs_low, values.reshape(shaped), precision=lax.Precision.HIGHEST).reshape(-1, D)
    attended = low_back(low(attended))
    branch = low_back(matmul_high(attended, w_o) + b_o)
    middle = layer_norm(flat_in + branch, ln1_gain, ln1_bias)
    upper = low_back(matmul_high(low(middle), w_in) + b_in)
    active = low(jax.nn.gelu(upper, approximate=False))
    down = low_back(matmul_high(active, w_out) + b_out)
    return layer_norm(middle + down, ln2_gain, ln2_bias).reshape(row_count, LEN, D)

def reference(hidden_in, w_qkv, b_qv, w_o, b_o, ln1_gain, ln1_bias, w_in, b_in, w_out, b_out, ln2_gain, ln2_bias, seg_lengths, cotangent):
    params = tuple((item.astype(jnp.float32) for item in (w_qkv, b_qv, w_o, b_o, ln1_gain, ln1_bias, w_in, b_in, w_out, b_out, ln2_gain, ln2_bias)))
    group = math.gcd(ROWS, max(1, 4096 // LEN))
    groups = ROWS // group
    positions = jnp.arange(LEN, dtype=jnp.int32)
    slots = jnp.arange(SEGS, dtype=jnp.int32)

    def one_group(carry, batch):
        inputs, lengths_in, grad_out = batch
        ids_row = segment_ids(lengths_in, positions)
        same_seg = ids_row[:, :, None] == ids_row[:, None, :]

        def run_layer(inputs_f, *weights):
            return forward(inputs_f, *weights, same_seg)
        final, pull = jax.vjp(run_layer, inputs.astype(jnp.float32), *params)
        grads = pull(grad_out.astype(jnp.float32))
        member = (ids_row[:, None, :] == slots[None, :, None]).astype(jnp.float32)
        pooled = jnp.einsum('rsp,rpd->rsd', member, final, precision=lax.Precision.HIGHEST)
        pooled = pooled / lengths_in[:, :, None].astype(jnp.float32)
        carry = tuple((total + extra for total, extra in zip(carry, grads[1:])))
        return (carry, (final.astype(jnp.bfloat16), pooled, grads[0]))
    start_sums = tuple((jnp.zeros_like(item) for item in params))
    batches = (hidden_in.reshape(groups, group, LEN, D), seg_lengths.reshape(groups, group, SEGS), cotangent.reshape(groups, group, LEN, D))
    sums, (output, pooled, d_input) = lax.scan(one_group, start_sums, batches)
    return (output.reshape(ROWS, LEN, D), pooled.reshape(ROWS, SEGS, D), d_input.reshape(ROWS, LEN, D), sums[0].reshape(-1), sums[2].reshape(-1), sums[6].reshape(-1), sums[8].reshape(-1), sums[1], sums[3], sums[4], sums[5], sums[7], sums[9], sums[10], sums[11])
```

```python
import functools
import math

import jax
import jax.numpy as jnp
from jax import lax
from jax.experimental import pallas as pl
from jax.experimental.pallas import tpu as pltpu
from jax.sharding import PartitionSpec as P

HEADS = 12
EPSILON = 1e-12
HIDE = -1e30
GROUPS = 16
BF = jnp.bfloat16
F32 = jnp.float32
VMEM_BYTES = 56 * 2**20


def sds(shape, dtype):
    return jax.ShapeDtypeStruct(shape, dtype)


def nn(left, right):
    return jnp.dot(left, right, preferred_element_type=F32)


def nt(left, right):
    return lax.dot_general(left, right, (((1,), (1,)), ((), ())), preferred_element_type=F32)


def tn(left, right):
    return lax.dot_general(left, right, (((0,), (0,)), ((), ())), preferred_element_type=F32)


def call(kernel, outs, *args, scratch=(), hbm=(), smem=(), flops=0, name=None):
    specs = []
    total = 0
    for i, arg in enumerate(args):
        total += arg.size * arg.dtype.itemsize
        if i in hbm:
            specs.append(pl.BlockSpec(memory_space=pl.ANY))
        elif i in smem:
            specs.append(pl.BlockSpec(memory_space=pltpu.SMEM))
        else:
            specs.append(pl.BlockSpec(memory_space=pltpu.VMEM))
    total += sum(math.prod(o.shape) * o.dtype.itemsize for o in outs)
    return pl.pallas_call(
        kernel,
        out_shape=list(outs),
        in_specs=specs,
        out_specs=[pl.BlockSpec(memory_space=pltpu.VMEM) for _ in outs],
        scratch_shapes=list(scratch),
        compiler_params=pltpu.CompilerParams(vmem_limit_bytes=VMEM_BYTES),
        cost_estimate=pl.CostEstimate(flops=flops, bytes_accessed=total, transcendentals=0),
        name=name,
    )(*args)


def segment_of(positions, lens_ref):
    ids = jnp.zeros_like(positions)
    end = jnp.int32(0)
    for j in range(lens_ref.shape[1]):
        end = end + lens_ref[0, j]
        ids = ids + (positions >= end).astype(jnp.int32)
    return ids


def own_first(index, half, s):
    return jnp.where(index < half, index + s * half, index - half + (1 - s) * half)


def normalise(total):
    centered = total - jnp.mean(total, axis=-1, keepdims=True)
    inverse = lax.rsqrt(jnp.mean(centered * centered, axis=-1, keepdims=True) + EPSILON)
    return centered * inverse, inverse


def norm_pull(grad, normal, inverse, gain):
    scaled = grad * gain
    return inverse * (
        scaled
        - jnp.mean(scaled, axis=-1, keepdims=True)
        - normal * jnp.mean(scaled * normal, axis=-1, keepdims=True)
    )


def column_sum(matrix):
    return jnp.sum(matrix, axis=0, keepdims=True)


def attend_kernel(
    lens, own, other, w_hbm, b_qv, q_out, k_out, v_out, kt_out, probs_out, att_out, w_buf, sems
):
    half, width = own.shape
    length = 2 * half
    mine = width // 2
    pair = 2 * (width // HEADS)
    head = pair // 2
    s = lax.axis_index("seq")
    copies = []
    for c in range(3):
        start = pl.multiple_of(c * width + s * mine, 128)
        copies.append(pltpu.make_async_copy(w_hbm.at[:, pl.ds(start, mine)], w_buf.at[c], sems.at[c]))
        copies[-1].start()
    column = pl.ds(pl.multiple_of(s * mine, 128), mine)
    bias = (b_qv[0:1, column].astype(F32), None, b_qv[1:2, column].astype(F32))
    parts = []
    for c in range(3):
        copies[c].wait()
        whole = []
        for tokens in (own, other):
            lin = nn(tokens[...], w_buf[c])
            if bias[c] is not None:
                lin = lin + bias[c]
            whole.append(lin)
        parts.append(jnp.concatenate(whole, axis=0))
    q_all, k_all, v_all = parts
    q_all = q_all.astype(BF).astype(F32) * (1.0 / math.sqrt(head))
    q_out[...] = q_all.astype(BF)
    k_out[...] = k_all.astype(BF)
    v_out[...] = v_all.astype(BF)
    kt_out[...] = k_all.T.astype(BF)
    vt = v_all.T.astype(BF)
    rows = own_first(lax.broadcasted_iota(jnp.int32, (length, pair), 0), half, s)
    lane = lax.broadcasted_iota(jnp.int32, (length, pair), 1)
    same = segment_of(rows, lens) == lane % head
    in_range = lane % head < lens.shape[1]
    mark_k = jnp.where(same, 1.0, 0.0)
    mark_q = jnp.where(jnp.logical_and(in_range, jnp.logical_not(same)), HIDE, 0.0)
    first = lane < head
    for j in range(mine // pair):
        cols = slice(j * pair, (j + 1) * pair)
        q2, k2 = q_all[:, cols], k_all[:, cols]
        pieces = []
        for a in range(2):
            keep = first if a == 0 else jnp.logical_not(first)
            k_m = jnp.where(keep, k2, mark_k).astype(BF)
            q_m = jnp.where(keep, q2, mark_q).astype(BF)
            scores = nt(k_m, q_m)
            top = jnp.max(scores, axis=0, keepdims=True)
            expo = jnp.exp(scores - top)
            total = jnp.sum(expo, axis=0, keepdims=True)
            probs = (expo * (1.0 / total)).astype(BF)
            h = 2 * j + a
            probs_out[h] = probs
            pieces.append(nn(vt[h * head : (h + 1) * head, :], probs))
        att_out[:, cols] = jnp.concatenate(pieces, axis=0).T.astype(BF)


def forward_kernel(
    lens,
    own,
    att_mine,
    att_got,
    w_o,
    b_o,
    gain1,
    shift1,
    w_in,
    b_in,
    w_out,
    b_out,
    gain2,
    shift2,
    cot,
    mid_out,
    active_out,
    pull_out,
    normal_out,
    inverse_out,
    sum2_out,
    down_keep,
    down_send,
    out_out,
    pool_out,
    vec_out,
    down_acc,
):
    half, width = own.shape
    mine = width // 2
    ff = w_in.shape[1]
    s = lax.axis_index("seq")
    row_a = pl.ds(pl.multiple_of(s * mine, 128), mine)
    row_b = pl.ds(pl.multiple_of((1 - s) * mine, 128), mine)
    branch = nn(att_mine[0:half, :], w_o[row_a, :]) + nn(att_got[half:, :], w_o[row_b, :])
    normal, inverse = normalise(own[...].astype(F32) + (branch + b_o[...].astype(F32)))
    middle = normal * gain1[...].astype(F32) + shift1[...].astype(F32)
    low = middle.astype(BF)
    mid_out[...] = low
    normal_out[...] = normal
    inverse_out[...] = inverse
    down_acc[...] = middle + b_out[...].astype(F32)
    step = 512
    for c in range(0, ff, step):
        cols = slice(c, c + step)
        upper = nn(low, w_in[:, cols]) + b_in[:, cols].astype(F32)
        cdf = 0.5 + 0.5 * lax.erf(upper * (1.0 / math.sqrt(2.0)))
        density = jnp.exp(-0.5 * upper * upper) * (1.0 / math.sqrt(2.0 * math.pi))
        act = (upper * cdf).astype(BF)
        active_out[:, cols] = act
        pull_out[:, cols] = cdf + upper * density
        down_acc[...] += nn(act, w_out[cols, :])
    normal2, inverse2 = normalise(down_acc[...])
    gain = gain2[...].astype(F32)
    final = normal2 * gain + shift2[...].astype(F32)
    out_out[...] = final.astype(BF)
    rows = lax.broadcasted_iota(jnp.int32, (half, width), 0) + s * half
    ids = segment_of(rows, lens)
    pool_out[...] = jnp.zeros_like(pool_out)
    for t in range(lens.shape[1]):
        pool_out[t : t + 1, :] = column_sum(jnp.where(ids == t, final, 0.0))
    grad = cot[...].astype(F32)
    sum2 = norm_pull(grad, normal2, inverse2, gain)
    sum2_out[...] = sum2
    down = sum2.astype(BF)
    down_acc[...] = sum2
    down_keep[...] = down_acc[:, row_a].astype(BF)
    down_send[...] = down_acc[:, row_b].astype(BF)
    vec_out[...] = jnp.zeros_like(vec_out)
    vec_out[0:1, :] = column_sum(grad * normal2)
    vec_out[1:2, :] = column_sum(grad)
    vec_out[2:3, :] = column_sum(down.astype(F32))


def backward_kernel(
    sum2, pull, normal, inverse, gain1, w_in, w_out,
    up_keep, up_send, sum1_out, branch_out, vec_out, mid_acc,
):
    width, ff = w_in.shape
    s = lax.axis_index("seq")
    step = 512
    per = ff // 2 // step
    mid_acc[...] = sum2[...]
    low = sum2[...].astype(BF)
    vec_out[...] = jnp.zeros_like(vec_out)
    sums = []
    for i in range(2 * per):
        block = (i // per + s) % 2
        start = pl.multiple_of(block * (ff // 2) + (i % per) * step, 128)
        cols = pl.ds(start, step)
        grad_upper = (nt(low, w_out[cols, :]) * pull[:, cols]).astype(BF)
        place = up_keep if i < per else up_send
        place[:, (i % per) * step : (i % per + 1) * step] = grad_upper
        sums.append(column_sum(grad_upper.astype(F32)))
        mid_acc[...] += nt(grad_upper, w_in[:, cols])
    ups = [jnp.concatenate(sums[:per], axis=1), jnp.concatenate(sums[per:], axis=1)]
    for b in range(2):
        line = jnp.where(s == b, ups[0], ups[1])
        for r in range(ff // 2 // width):
            row = b * (ff // 2 // width) + r
            vec_out[row : row + 1, :] = line[:, r * width : (r + 1) * width]
    base = ff // width
    grad_mid = mid_acc[...]
    vec_out[base : base + 1, :] = column_sum(grad_mid * normal[...])
    vec_out[base + 1 : base + 2, :] = column_sum(grad_mid)
    sum1 = norm_pull(grad_mid, normal[...], inverse[...], gain1[...].astype(F32))
    sum1_out[...] = sum1
    branch = sum1.astype(BF)
    branch_out[...] = branch
    vec_out[base + 2 : base + 3, :] = column_sum(branch.astype(F32))


def attend_back_kernel(
    branch_own, branch_got, w_o, q, k, v, kt, probs, grad_out, vec_out
):
    length, mine = q.shape
    width = w_o.shape[1]
    head = width // HEADS
    pair = 2 * head
    s = lax.axis_index("seq")
    w_mine = w_o[pl.ds(pl.multiple_of(s * mine, 128), mine), :]
    att_t = jnp.concatenate(
        [nt(w_mine, branch_own[...]).astype(BF), nt(w_mine, branch_got[...]).astype(BF)], axis=1
    )
    lane = lax.broadcasted_iota(jnp.int32, (length, pair), 1)
    first = lane < head
    vec_out[...] = jnp.zeros_like(vec_out)
    for j in range(mine // pair):
        cols = slice(j * pair, (j + 1) * pair)
        q2 = q[:, cols]
        v2 = v[:, cols].astype(F32)
        a2 = att_t[cols, :]
        dq, dk, dv = [], [], []
        for a in range(2):
            h = 2 * j + a
            keep = first if a == 0 else jnp.logical_not(first)
            v_m = jnp.where(keep, v2, 0.0).astype(BF)
            grad_p = nn(v_m, a2)
            low = probs[h]
            prob = low.astype(F32)
            inner = jnp.sum(prob * grad_p, axis=0, keepdims=True)
            raw = (prob * (grad_p - inner)).astype(BF)
            dk.append(nn(raw, q2))
            dv.append(nt(low, a2))
            dq.append(nn(kt[h * head : (h + 1) * head, :], raw))
        dq_low = (jnp.concatenate(dq, axis=0) * (1.0 / math.sqrt(head))).T.astype(BF)
        dk_low = jnp.where(first, dk[0], dk[1]).astype(BF)
        dv_low = jnp.where(first, dv[0], dv[1]).astype(BF)
        grad_out[:, cols] = dq_low
        grad_out[:, mine + j * pair : mine + (j + 1) * pair] = dk_low
        grad_out[:, 2 * mine + j * pair : 2 * mine + (j + 1) * pair] = dv_low
        vec_out[0:1, cols] = column_sum(dq_low.astype(F32))
        vec_out[1:2, cols] = column_sum(dv_low.astype(F32))


def slot_of(chunk, order):
    if order is None:
        return jnp.int32(chunk)
    rel = jnp.bitwise_xor(jnp.int32(chunk), lax.axis_index("dp"))
    s = lax.axis_index("seq")
    slots = []
    for bits in order:
        slot = jnp.int32(0)
        for bit in bits:
            slot = slot * 2 + jnp.bitwise_and(lax.shift_right_logical(rel, jnp.int32(bit)), 1)
        slots.append(slot)
    return jnp.where(s == 0, slots[0], slots[1])


def place(values, chunk, order, keep, send, cols=None):
    half = GROUPS // 2
    slot = slot_of(chunk, order)
    rows = values.shape[0]
    if cols is None:
        cols = slice(0, values.shape[1])

    def at(index):
        return pl.ds(pl.multiple_of(index * rows, 16), rows)

    @pl.when(slot < half)
    def _():
        keep[at(slot), cols] = values

    @pl.when(slot >= half)
    def _():
        send[at(slot - half), cols] = values


def grad_out_kernel(order, active_own, active_got, down_own, down_got, keep, send):
    ff = active_own.shape[1]
    rows = ff // GROUPS
    block = 2 * rows
    for i in range(GROUPS // 2):
        cols = slice(i * block, (i + 1) * block)
        got = (
            tn(active_own[:, cols], down_own[...]) + tn(active_got[:, cols], down_got[...])
        ).astype(BF)
        for b in range(2):
            place(got[b * rows : (b + 1) * rows, :], 2 * i + b, order, keep, send)


def grad_in_kernel(order, mid_own, mid_got, up_own, up_got, keep, send):
    width = mid_own.shape[1]
    rows = width // GROUPS
    for i in range(2):
        cols = slice(i * width // 2, (i + 1) * width // 2)
        for n in range(0, up_own.shape[1], 512):
            out = slice(n, n + 512)
            got = (
                tn(mid_own[:, cols], up_own[:, out]) + tn(mid_got[:, cols], up_got[:, out])
            ).astype(BF)
            for b in range(GROUPS // 2):
                place(
                    got[b * rows : (b + 1) * rows, :], i * (GROUPS // 2) + b, order, keep, send, out
                )


def grad_qkv_kernel(
    order, own, other, grads, att_mine, att_got, branch_own, branch_got, vec_f, vec_b, vec_a,
    keep, send, vec_keep,
):
    half, width = own.shape
    mine = width // 2
    rows = width // GROUPS
    s = lax.axis_index("seq")
    column = pl.ds(pl.multiple_of(s * mine, 128), mine)
    for i in range(2):
        cols = slice(i * mine, (i + 1) * mine)
        for c in range(3):
            out = slice(c * mine, (c + 1) * mine)
            got = (tn(own[:, cols], grads[0:half, out]) + tn(other[:, cols], grads[half:, out])).astype(BF)
            for b in range(GROUPS // 2):
                place(got[b * rows : (b + 1) * rows, :], i * (GROUPS // 2) + b, order, keep, send, out)
    out = slice(3 * mine, 4 * mine)
    mine_o = tn(att_mine[0:half, :], branch_own[:, column]) + tn(att_mine[half:, :], branch_got[:, column])
    got_o = tn(att_got[half:, :], branch_own[:, column]) + tn(att_got[0:half, :], branch_got[:, column])
    for i in range(2):
        got = jnp.where(s == i, mine_o, got_o).astype(BF)
        for b in range(GROUPS // 2):
            place(got[b * rows : (b + 1) * rows, :], i * (GROUPS // 2) + b, order, keep, send, out)
    base = vec_b.shape[0]
    zero = jnp.zeros((1, mine), F32)
    lines = []
    for r in range(2):
        line = vec_a[r : r + 1, :]
        lines.append(
            jnp.concatenate([jnp.where(s == 0, line, zero), jnp.where(s == 0, zero, line)], axis=1)
        )
    table = jnp.concatenate(lines + [vec_b[0:7, :], vec_f[0:3, :], jnp.zeros((4, width), F32)], axis=0)
    high = table.astype(BF)
    rest = (table - high.astype(F32)).astype(BF)
    extra = slice(GROUPS // 2 * rows, GROUPS // 2 * rows + 16)
    send[extra, 0:width] = high
    send[extra, width:] = rest
    vec_keep[...] = high.astype(F32) + rest.astype(F32)


def merge_kernel(rows, got, keep, keep_out, send_out):
    total = keep[0:rows, :].astype(F32) + got[0:rows, :].astype(F32)
    keep_out[...] = total[0 : rows // 2, :].astype(BF)
    send_out[...] = total[rows // 2 :, :].astype(BF)


def merge_vec_kernel(rows, got, keep, vec, keep_out, send_out, vec_out):
    width = vec.shape[1]
    merge_kernel(rows, got, keep, keep_out, send_out.at[0 : rows // 2, :])
    table = vec[...] + (got[rows:, 0:width].astype(F32) + got[rows:, width:].astype(F32))
    high = table.astype(BF)
    rest = (table - high.astype(F32)).astype(BF)
    extra = slice(rows // 2, rows // 2 + 16)
    send_out[extra, 0:width] = high
    send_out[extra, width:] = rest
    vec_out[...] = high.astype(F32) + rest.astype(F32)


def last_kernel(got, keep, keep_out, send_out, acc):
    rows = keep.shape[0]
    s = lax.axis_index("seq")
    acc[...] = keep[...].astype(F32) + got[0:rows, :].astype(F32)
    keep_out[...] = acc[pl.ds(pl.multiple_of(s * (rows // 2), 8), rows // 2), :]
    send_out[...] = acc[pl.ds(pl.multiple_of((1 - s) * (rows // 2), 8), rows // 2), :]


def last_vec_kernel(got, keep, vec, keep_out, send_out, acc):
    rows = keep.shape[0]
    width = vec.shape[1]
    last_kernel(got, keep, keep_out, send_out.at[0 : rows // 2, :], acc)
    table = vec[...] + (got[rows:, 0:width].astype(F32) + got[rows:, width:].astype(F32))
    send_out[rows // 2 :, 0:width] = table
    send_out[rows // 2 :, width:] = jnp.zeros_like(table)


def swap(x, axis="seq"):
    return lax.ppermute(x, axis, [(0, 1), (1, 0)])


def send_to(x, phase, order, count):
    pairs = []
    for d in range(count):
        for s in range(2):
            pairs.append((2 * d + s, 2 * (d ^ (1 << order[s][phase])) + s))
    return lax.ppermute(x, ("dp", "seq"), pairs)


def reduce_rows(keep, send, order, count, name, vec=None):
    phases = len(order[0])
    rows = keep.shape[0]
    cols = keep.shape[1]
    for p in range(phases - 1):
        got = send_to(send, p, order, count)
        if vec is None:
            keep, send = call(
                functools.partial(merge_kernel, rows),
                [sds((rows // 2, cols), BF), sds((rows // 2, cols), BF)],
                got, keep, name=f"{name}_merge{p}",
            )
        else:
            keep, send, vec = call(
                functools.partial(merge_vec_kernel, rows),
                [sds((rows // 2, cols), BF), sds((rows // 2 + 16, cols), BF), sds(vec.shape, F32)],
                got, keep, vec, name=f"{name}_merge{p}",
            )
        rows //= 2
    got = send_to(send, phases - 1, order, count)
    scratch = [pltpu.VMEM((rows, cols), F32)]
    if vec is None:
        return call(
            last_kernel,
            [sds((rows // 2, cols), F32), sds((rows // 2, cols), F32)],
            got, keep, scratch=scratch, name=f"{name}_last",
        )
    return call(
        last_vec_kernel,
        [sds((rows // 2, cols), F32), sds((rows // 2 + 16, cols), F32)],
        got, keep, vec, scratch=scratch, name=f"{name}_last",
    )


def interleave(keep, got, s, pieces):
    size = keep.shape[1] // pieces
    outs = []
    for i in range(pieces):
        a, b = keep[:, i * size : (i + 1) * size], got[:, i * size : (i + 1) * size]
        outs += [jnp.where(s == 0, a, b), jnp.where(s == 0, b, a)]
    return outs


def on_device(
    orders, count,
    hidden_in, w_qkv, b_qv, w_o, b_o, ln1_gain, ln1_bias, w_in, b_in, w_out, b_out, ln2_gain, ln2_bias,
    seg_lengths, cotangent,
):
    row_count, half, width = hidden_in.shape
    length = 2 * half
    mine = width // 2
    heads = HEADS // 2
    ff = w_in.shape[1]
    s = lax.axis_index("seq")
    order_out, order_in, order_qkv = orders if orders else (None, None, None)
    own = hidden_in.reshape(half, width)
    cot = cotangent.reshape(half, width)
    line = lambda x: x.reshape(1, -1)
    other = swap(own)
    q, k, v, kt, probs, att_mine = call(
        attend_kernel,
        [sds((length, mine), BF)] * 3
        + [sds((mine, length), BF), sds((heads, length, length), BF), sds((length, mine), BF)],
        seg_lengths, own, other, w_qkv, b_qv,
        smem=(0,), hbm=(3,),
        scratch=[pltpu.VMEM((3, width, mine), BF), pltpu.SemaphoreType.DMA((3,))],
        flops=2 * length * width * 3 * mine + 4 * heads * length * length * 256,
        name="attend",
    )
    att_got = swap(att_mine)
    (mid_low, active, pull, normal, inverse, sum2, down_own, down_send, output, pool_part, vec_f) = call(
        forward_kernel,
        [
            sds((half, width), BF), sds((half, ff), BF), sds((half, ff), F32), sds((half, width), F32),
            sds((half, 1), F32), sds((half, width), F32), sds((half, mine), BF), sds((half, mine), BF),
            sds((half, width), BF), sds((8, width), F32), sds((8, width), F32),
        ],
        seg_lengths, own, att_mine, att_got, w_o, line(b_o), line(ln1_gain), line(ln1_bias), w_in, line(b_in),
        w_out, line(b_out), line(ln2_gain), line(ln2_bias), cot,
        smem=(0,), scratch=[pltpu.VMEM((half, width), F32)],
        flops=2 * half * (width * width + 2 * width * ff), name="forward",
    )
    active_got = swap(active)
    mid_got = swap(mid_low)
    down_got = swap(down_send)
    up_own, up_send, sum1, branch_own, vec_b = call(
        backward_kernel,
        [
            sds((half, ff // 2), BF), sds((half, ff // 2), BF), sds((half, width), F32),
            sds((half, width), BF), sds((8, width), F32),
        ],
        sum2, pull, normal, inverse, line(ln1_gain), w_in, w_out,
        scratch=[pltpu.VMEM((half, width), F32)],
        flops=4 * half * width * ff, name="backward",
    )
    branch_got = swap(branch_own)
    up_got = swap(up_send)
    rows_ff, rows_w = ff // GROUPS, width // GROUPS
    keep_out, send_out = call(
        functools.partial(grad_out_kernel, order_out),
        [sds((GROUPS // 2 * rows_ff, mine), BF)] * 2,
        active, active_got, down_own, down_got,
        flops=2 * length * ff * mine, name="grad_out",
    )
    keep_in, send_in = call(
        functools.partial(grad_in_kernel, order_in),
        [sds((GROUPS // 2 * rows_w, ff // 2), BF)] * 2,
        mid_low, mid_got, up_own, up_got,
        flops=2 * length * width * ff // 2, name="grad_in",
    )
    grads, vec_a = call(
        attend_back_kernel,
        [sds((length, 3 * mine), BF), sds((8, mine), F32)],
        branch_own, branch_got, w_o, q, k, v, kt, probs,
        flops=2 * length * width * mine + 10 * heads * length * length * 256, name="attend_back",
    )
    keep_qkv, send_qkv, vec = call(
        functools.partial(grad_qkv_kernel, order_qkv),
        [sds((GROUPS // 2 * rows_w, 4 * mine), BF), sds((GROUPS // 2 * rows_w + 16, 4 * mine), BF), sds((16, width), F32)],
        own, other, grads, att_mine, att_got, branch_own, branch_got, vec_f, vec_b, vec_a,
        flops=2 * length * width * 4 * mine, name="grad_qkv",
    )

    def grad_input_kernel(grads, w_hbm, sum1, pool, keep_ref, send_ref, w_buf, sems):
        core = lax.axis_index("seq")
        copies = []
        for c in range(3):
            start = pl.multiple_of(c * width + core * mine, 128)
            copies.append(
                pltpu.make_async_copy(w_hbm.at[:, pl.ds(start, mine)], w_buf.at[c], sems.at[c])
            )
            copies[-1].start()
        a, b = sum1[...], jnp.zeros((half, width), F32)
        for c in range(3):
            copies[c].wait()
            cols = slice(c * mine, (c + 1) * mine)
            a = a + nt(grads[0:half, cols], w_buf[c])
            b = b + nt(grads[half:, cols], w_buf[c])
        keep_ref[...] = a
        send_ref[0:half, :] = b
        send_ref[half:, :] = pool[...]

    input_keep, input_send = call(
        grad_input_kernel,
        [sds((half, width), F32), sds((half + 8, width), F32)],
        grads, w_qkv, sum1, pool_part,
        hbm=(1,), scratch=[pltpu.VMEM((3, width, mine), BF), pltpu.SemaphoreType.DMA((3,))],
        flops=2 * length * width * 3 * mine, name="grad_input",
    )
    input_got = swap(input_send)
    d_input = input_keep + input_got[:half]
    pool_sum = (pool_part + input_got[half:])[: seg_lengths.shape[1]]
    pooled = pool_sum / seg_lengths.reshape(-1, 1).astype(F32)

    if orders:
        out_keep, out_send = reduce_rows(keep_out, send_out, order_out, count, "out")
        in_keep, in_send = reduce_rows(keep_in, send_in, order_in, count, "in")
        qkv_keep, qkv_send = reduce_rows(keep_qkv, send_qkv, order_qkv, count, "qkv", vec)
        out_got, in_got, qkv_got = swap(out_send), swap(in_send), swap(qkv_send)
        rows = qkv_keep.shape[0]
        vec = qkv_send[rows:, :width] + qkv_got[rows:, :width]
        qkv_got = qkv_got[:rows]
    else:
        done = []
        for keep, send in ((keep_out, send_out), (keep_in, send_in), (keep_qkv, send_qkv)):
            both = jnp.concatenate([keep, send[: keep.shape[0]]], axis=0)
            total = lax.psum_scatter(both, "dp", scatter_dimension=0, tiled=True).astype(F32)
            parts = total.reshape(2, -1, total.shape[1])
            done.append((jnp.where(s == 0, parts[0], parts[1]), swap(jnp.where(s == 0, parts[1], parts[0]))))
        (out_keep, out_got), (in_keep, in_got), (qkv_keep, qkv_got) = done
        vec = lax.psum(vec, ("dp", "seq"))
    flat_out = jnp.concatenate(interleave(out_keep, out_got, s, 1), axis=1).reshape(-1)
    flat_in = jnp.concatenate(interleave(in_keep, in_got, s, 1), axis=1).reshape(-1)
    pieces = interleave(qkv_keep, qkv_got, s, 4)
    flat_qkv = jnp.concatenate(pieces[:6], axis=1).reshape(-1)
    flat_o = jnp.concatenate(pieces[6:], axis=1).reshape(-1)
    base = ff // width
    return (
        output.reshape(row_count, half, width),
        pooled[None],
        d_input.reshape(row_count, half, width),
        flat_qkv,
        flat_o,
        flat_in,
        flat_out,
        vec[0:2],
        vec[2 + base + 2],
        vec[2 + base],
        vec[2 + base + 1],
        vec[2 : 2 + base].reshape(-1),
        vec[2 + base + 5],
        vec[2 + base + 3],
        vec[2 + base + 4],
    )


def solution(mesh):
    count = mesh.shape["dp"]
    orders = None
    if count == GROUPS:
        orders = (
            ((0, 2, 3, 1), (1, 2, 3, 0)),
            ((0, 1, 2, 3), (1, 0, 2, 3)),
            ((0, 1, 2, 3), (1, 0, 2, 3)),
        )
    in_specs = (P("dp", "seq", None),) + (P(),) * 12 + (P("dp", None), P("dp", "seq", None))
    out_specs = (
        P("dp", "seq", None),
        P("dp", None, None),
        P("dp", "seq", None),
    ) + (P(("dp", "seq")),) * 4 + (P(),) * 8
    return jax.shard_map(
        functools.partial(on_device, orders, count),
        mesh=mesh, in_specs=in_specs, out_specs=out_specs, check_vma=False,
    )
```

```python
import functools
import math

import jax
import jax.numpy as jnp
from jax import lax
from jax.experimental import pallas as pl
from jax.experimental.pallas import tpu as pltpu
from jax.sharding import PartitionSpec as P

HEADS = 12
EPSILON = 1e-12
HIDE = -1e30
GROUPS = 16
BF = jnp.bfloat16
F32 = jnp.float32
MIB = 2**20
MERGE_US = 0.3
KERNEL_US = 0.3
WEIGHTS = {"out": 1, "in": 1, "qkv": 3, "o": 1}
PARTS = {
    "a": ("out", 0, 384, "xy12"),
    "b": ("in", 0, 768, "xy12"),
    "c": ("in", 768, 1536, "1xy2"),
    "d": ("qkv", 0, 384, "12xy"),
    "e": ("qkv", 384, 1152, "yx12"),
}
WITH_O = "c"
WITH_VECTORS = "d"
PLAN = (
    "BWD", "OUT", "IN", "BACK", "out", "QKV", "INPUT", "in", "out", "qkv", "input", "in",
    "out", "qkv", "in", "out", "qkv", "in", "qkv",
)


def sds(shape, dtype):
    return jax.ShapeDtypeStruct(shape, dtype)


def nn(left, right):
    return jnp.dot(left, right, preferred_element_type=F32)


def nt(left, right):
    return lax.dot_general(left, right, (((1,), (1,)), ((), ())), preferred_element_type=F32)


def tn(left, right):
    return lax.dot_general(left, right, (((0,), (0,)), ((), ())), preferred_element_type=F32)


class Line:
    def __init__(self):
        self.last = None

    def call(self, kernel, outs, *args, scratch=(), hbm=(), smem=(), name=None, vmem=16, us=KERNEL_US, end=False):
        if end:
            outs = [sds((8, 128), F32), *outs]
        specs = []
        lead = len(args)
        for i in range(lead):
            space = pltpu.HBM if i in hbm else pltpu.SMEM if i in smem else pltpu.VMEM
            specs.append(pl.BlockSpec(memory_space=space))
        args = [
            pltpu.with_memory_space_constraint(arg, pltpu.HBM) if i in hbm else arg
            for i, arg in enumerate(args)
        ]
        after = () if self.last is None else (self.last,)
        specs += [pl.BlockSpec(memory_space=pl.ANY) for _ in after]

        def body(*refs):
            rest = refs[lead + len(after) :]
            if end:
                rest[0][...] = jnp.zeros((8, 128), F32)
                rest = rest[1:]
            kernel(*refs[:lead], *rest)

        made = pl.pallas_call(
            body,
            out_shape=list(outs),
            in_specs=specs,
            out_specs=[pl.BlockSpec(memory_space=pltpu.VMEM) for _ in outs],
            scratch_shapes=list(scratch),
            compiler_params=pltpu.CompilerParams(vmem_limit_bytes=vmem * MIB),
            cost_estimate=pl.CostEstimate(flops=int(us * 1.1e9), bytes_accessed=1024, transcendentals=0),
            name=name,
        )(*args, *after)
        self.last = made[0]
        return made[1:] if end else made


def segment_of(positions, lens_ref):
    ids = jnp.zeros_like(positions)
    end = jnp.int32(0)
    for j in range(lens_ref.shape[1]):
        end = end + lens_ref[0, j]
        ids = ids + (positions >= end).astype(jnp.int32)
    return ids


def own_first(index, half, s):
    return jnp.where(index < half, index + s * half, index - half + (1 - s) * half)


def normalise(total):
    centered = total - jnp.mean(total, axis=-1, keepdims=True)
    inverse = lax.rsqrt(jnp.mean(centered * centered, axis=-1, keepdims=True) + EPSILON)
    return centered * inverse, inverse


def norm_pull(grad, normal, inverse, gain):
    scaled = grad * gain
    return inverse * (
        scaled
        - jnp.mean(scaled, axis=-1, keepdims=True)
        - normal * jnp.mean(scaled * normal, axis=-1, keepdims=True)
    )


def column_sum(matrix):
    return jnp.sum(matrix, axis=0, keepdims=True)


def project_kernel(own_hbm, w_hbm, b_hbm, own, w_mine, bias, lin, b_buf, sems):
    width = own.shape[1]
    mine = width // 2
    s = lax.axis_index("seq")
    first = pltpu.make_async_copy(own_hbm, own, sems.at[3])
    first.start()
    copies = []
    for c in range(3):
        start = pl.multiple_of(c * width + s * mine, 128)
        copies.append(pltpu.make_async_copy(w_hbm.at[:, pl.ds(start, mine)], w_mine.at[c], sems.at[c]))
        copies[-1].start()
    second = pltpu.make_async_copy(b_hbm, b_buf, sems.at[4])
    second.start()
    second.wait()
    column = pl.ds(pl.multiple_of(s * mine, 128), mine)
    bias[...] = jnp.zeros_like(bias)
    bias[0:1, :] = b_buf[0:1, column].astype(F32)
    bias[2:3, :] = b_buf[1:2, column].astype(F32)
    first.wait()
    for c in range(3):
        copies[c].wait()
        lin[:, c * mine : (c + 1) * mine] = nn(own[...], w_mine[c]) + bias[c : c + 1, :]


def attend_kernel(
    lens, other, w_mine, bias, lin, w_o_hbm, w_in_hbm, w_out_hbm,
    q_out, k_out, v_out, kt_out, expo_out, scale_out, att_t, att_out, w_o, w_in, w_out, sems,
):
    half, width = other.shape
    length = 2 * half
    mine = width // 2
    pair = 2 * (width // HEADS)
    head = pair // 2
    s = lax.axis_index("seq")
    copies = [
        pltpu.make_async_copy(source, target, sems.at[i])
        for i, (source, target) in enumerate(((w_o_hbm, w_o), (w_in_hbm, w_in), (w_out_hbm, w_out)))
    ]
    for copy in copies:
        copy.start()
    parts = []
    for c in range(3):
        rest = nn(other[...], w_mine[c]) + bias[c : c + 1, :]
        parts.append(jnp.concatenate([lin[:, c * mine : (c + 1) * mine], rest], axis=0))
    q_all, k_all, v_all = parts
    q_all = q_all.astype(BF).astype(F32) * (1.0 / math.sqrt(head))
    q_out[...] = q_all.astype(BF)
    k_out[...] = k_all.astype(BF)
    v_out[...] = v_all.astype(BF)
    kt_out[...] = k_all.T.astype(BF)
    vt = v_all.T.astype(BF)
    rows = own_first(lax.broadcasted_iota(jnp.int32, (length, pair), 0), half, s)
    lane = lax.broadcasted_iota(jnp.int32, (length, pair), 1)
    same = segment_of(rows, lens) == lane % head
    in_range = lane % head < lens.shape[1]
    mark_k = jnp.where(same, 1.0, 0.0)
    mark_q = jnp.where(jnp.logical_and(in_range, jnp.logical_not(same)), HIDE, 0.0)
    first = lane < head
    for j in range(mine // pair):
        cols = slice(j * pair, (j + 1) * pair)
        q2, k2 = q_all[:, cols], k_all[:, cols]
        pieces = []
        for a in range(2):
            keep = first if a == 0 else jnp.logical_not(first)
            k_m = jnp.where(keep, k2, mark_k).astype(BF)
            q_m = jnp.where(keep, q2, mark_q).astype(BF)
            scores = nt(k_m, q_m)
            top = jnp.max(scores, axis=0, keepdims=True)
            expo = jnp.exp(scores - top)
            scale = 1.0 / jnp.sum(expo, axis=0, keepdims=True)
            low = expo.astype(BF)
            h = 2 * j + a
            expo_out[h] = low
            scale_out[h : h + 1, :] = scale
            pieces.append(nn(vt[h * head : (h + 1) * head, :], low) * scale)
        both = jnp.concatenate(pieces, axis=0)
        att_t[cols, :] = both
        att_out[:, cols] = both.T.astype(BF)
    for copy in copies:
        copy.wait()


def forward_kernel(
    lens,
    own,
    att_mine,
    att_got,
    w_o,
    b_o,
    gain1,
    shift1,
    w_in,
    b_in,
    w_out,
    b_out,
    gain2,
    shift2,
    cot,
    mid_out,
    active_out,
    pull_out,
    normal_out,
    inverse_out,
    sum2_out,
    down_keep,
    down_send,
    out_out,
    pool_out,
    vec_out,
    down_acc,
):
    half, width = own.shape
    mine = width // 2
    ff = w_in.shape[1]
    s = lax.axis_index("seq")
    row_a = pl.ds(pl.multiple_of(s * mine, 128), mine)
    row_b = pl.ds(pl.multiple_of((1 - s) * mine, 128), mine)
    branch = nn(att_mine[0:half, :], w_o[row_a, :]) + nn(att_got[half:, :], w_o[row_b, :])
    normal, inverse = normalise(own[...].astype(F32) + (branch + b_o[...].astype(F32)))
    middle = normal * gain1[...].astype(F32) + shift1[...].astype(F32)
    low = middle.astype(BF)
    mid_out[...] = low
    normal_out[...] = normal
    inverse_out[...] = inverse
    down_acc[...] = middle + b_out[...].astype(F32)
    step = 1024
    for c in range(0, ff, step):
        cols = slice(c, c + step)
        upper = nn(low, w_in[:, cols]) + b_in[:, cols].astype(F32)
        cdf = 0.5 + 0.5 * lax.erf(upper * (1.0 / math.sqrt(2.0)))
        density = jnp.exp(-0.5 * upper * upper) * (1.0 / math.sqrt(2.0 * math.pi))
        act = (upper * cdf).astype(BF)
        active_out[:, cols] = act
        pull_out[:, cols] = cdf + upper * density
        down_acc[...] += nn(act, w_out[cols, :])
    normal2, inverse2 = normalise(down_acc[...])
    gain = gain2[...].astype(F32)
    final = normal2 * gain + shift2[...].astype(F32)
    out_out[...] = final.astype(BF)
    rows = lax.broadcasted_iota(jnp.int32, (half, width), 0) + s * half
    ids = segment_of(rows, lens)
    pool_out[...] = jnp.zeros_like(pool_out)
    for t in range(lens.shape[1]):
        pool_out[t : t + 1, :] = column_sum(jnp.where(ids == t, final, 0.0))
    grad = cot[...].astype(F32)
    sum2 = norm_pull(grad, normal2, inverse2, gain)
    sum2_out[...] = sum2
    down = sum2.astype(BF)
    down_acc[...] = sum2
    down_keep[...] = down_acc[:, row_a].astype(BF)
    down_send[...] = down_acc[:, row_b].astype(BF)
    vec_out[...] = jnp.zeros_like(vec_out)
    vec_out[0:1, :] = column_sum(grad * normal2)
    vec_out[1:2, :] = column_sum(grad)
    vec_out[2:3, :] = column_sum(down.astype(F32))


def backward_kernel(
    sum2, pull, normal, inverse, gain1, w_in, w_out,
    up_keep, up_send, sum1_out, branch_out, vec_out, mid_acc,
):
    width, ff = w_in.shape
    s = lax.axis_index("seq")
    step = 768
    per = ff // 2 // step
    mid_acc[...] = sum2[...]
    low = sum2[...].astype(BF)
    vec_out[...] = jnp.zeros_like(vec_out)
    sums = []
    for i in range(2 * per):
        block = (i // per + s) % 2
        start = pl.multiple_of(block * (ff // 2) + (i % per) * step, 128)
        cols = pl.ds(start, step)
        grad_upper = (nt(low, w_out[cols, :]) * pull[:, cols]).astype(BF)
        place = up_keep if i < per else up_send
        place[:, (i % per) * step : (i % per + 1) * step] = grad_upper
        sums.append(column_sum(grad_upper.astype(F32)))
        mid_acc[...] += nt(grad_upper, w_in[:, cols])
    ups = [jnp.concatenate(sums[:per], axis=1), jnp.concatenate(sums[per:], axis=1)]
    for b in range(2):
        line = jnp.where(s == b, ups[0], ups[1])
        for r in range(ff // 2 // width):
            row = b * (ff // 2 // width) + r
            vec_out[row : row + 1, :] = line[:, r * width : (r + 1) * width]
    base = ff // width
    grad_mid = mid_acc[...]
    vec_out[base : base + 1, :] = column_sum(grad_mid * normal[...])
    vec_out[base + 1 : base + 2, :] = column_sum(grad_mid)
    sum1 = norm_pull(grad_mid, normal[...], inverse[...], gain1[...].astype(F32))
    sum1_out[...] = sum1
    branch = sum1.astype(BF)
    branch_out[...] = branch
    vec_out[base + 2 : base + 3, :] = column_sum(branch.astype(F32))


def attend_back_kernel(
    branch_own, branch_got, w_o, q, k, v, kt, expo, scale, att_t, grad_out, vec_out
):
    length, mine = q.shape
    width = w_o.shape[1]
    head = width // HEADS
    pair = 2 * head
    s = lax.axis_index("seq")
    w_mine = w_o[pl.ds(pl.multiple_of(s * mine, 128), mine), :]
    grad_t = jnp.concatenate([nt(w_mine, branch_own[...]), nt(w_mine, branch_got[...])], axis=1)
    lane = lax.broadcasted_iota(jnp.int32, (length, pair), 1)
    first = lane < head
    vec_out[...] = jnp.zeros_like(vec_out)
    for j in range(mine // pair):
        cols = slice(j * pair, (j + 1) * pair)
        q2 = q[:, cols]
        v2 = v[:, cols].astype(F32)
        scaled, inners = [], []
        for h in (2 * j, 2 * j + 1):
            part = slice(h * head, (h + 1) * head)
            times = scale[h : h + 1, :]
            scaled.append(grad_t[part, :] * times)
            inners.append(jnp.sum(att_t[part, :] * scaled[-1], axis=0, keepdims=True))
        a2 = jnp.concatenate(scaled, axis=0).astype(BF)
        dq, dk, dv = [], [], []
        for a in range(2):
            h = 2 * j + a
            keep = first if a == 0 else jnp.logical_not(first)
            v_m = jnp.where(keep, v2, 0.0).astype(BF)
            grad_p = nn(v_m, a2)
            low = expo[h]
            raw = (low.astype(F32) * (grad_p - inners[a])).astype(BF)
            dk.append(nn(raw, q2))
            dv.append(nt(low, a2))
            dq.append(nn(kt[h * head : (h + 1) * head, :], raw))
        dq_low = (jnp.concatenate(dq, axis=0) * (1.0 / math.sqrt(head))).T.astype(BF)
        dk_low = jnp.where(first, dk[0], dk[1]).astype(BF)
        dv_low = jnp.where(first, dv[0], dv[1]).astype(BF)
        grad_out[:, cols] = dq_low
        grad_out[:, mine + j * pair : mine + (j + 1) * pair] = dk_low
        grad_out[:, 2 * mine + j * pair : 2 * mine + (j + 1) * pair] = dv_low
        vec_out[0:1, cols] = column_sum(dq_low.astype(F32))
        vec_out[1:2, cols] = column_sum(dv_low.astype(F32))


def slot_of(chunk, order):
    if order is None:
        return jnp.int32(chunk)
    rel = jnp.bitwise_xor(jnp.int32(chunk), lax.axis_index("dp"))
    s = lax.axis_index("seq")
    slots = []
    for bits in order:
        slot = jnp.int32(0)
        for bit in bits:
            slot = slot * 2 + jnp.bitwise_and(lax.shift_right_logical(rel, jnp.int32(bit)), 1)
        slots.append(slot)
    return jnp.where(s == 0, slots[0], slots[1])


def place(values, chunk, order, keep, send, cols=None):
    half = GROUPS // 2
    slot = slot_of(chunk, order)
    rows = values.shape[0]
    if cols is None:
        cols = slice(0, values.shape[1])

    def at(index):
        return pl.ds(pl.multiple_of(index * rows, 16), rows)

    @pl.when(slot < half)
    def _():
        keep[at(slot), cols] = values

    @pl.when(slot >= half)
    def _():
        send[at(slot - half), cols] = values


def grad_out_kernel(parts, active_own, active_got, down_own, down_got, *outs):
    ff = active_own.shape[1]
    rows = ff // GROUPS
    block = 2 * rows
    for i in range(GROUPS // 2):
        cols = slice(i * block, (i + 1) * block)
        got = (
            tn(active_own[:, cols], down_own[...]) + tn(active_got[:, cols], down_got[...])
        ).astype(BF)
        for b in range(2):
            for p, (start, stop, order) in enumerate(parts):
                values = got[b * rows : (b + 1) * rows, start:stop]
                place(values, 2 * i + b, order, outs[2 * p], outs[2 * p + 1])


def grad_in_kernel(
    parts, with_o, mid_own, mid_got, up_own, up_got, att_mine, att_got, branch_own, branch_got, *outs
):
    half, width = mid_own.shape
    mine = width // 2
    rows = width // GROUPS
    for i in range(2):
        cols = slice(i * mine, (i + 1) * mine)
        for p, (start, stop, order) in enumerate(parts):
            for n in range(start, stop, 512):
                out = slice(n, min(n + 512, stop))
                got = (
                    tn(mid_own[:, cols], up_own[:, out]) + tn(mid_got[:, cols], up_got[:, out])
                ).astype(BF)
                to = slice(n - start, out.stop - start)
                for b in range(GROUPS // 2):
                    place(
                        got[b * rows : (b + 1) * rows, :], i * (GROUPS // 2) + b, order,
                        outs[2 * p], outs[2 * p + 1], to,
                    )
    s = lax.axis_index("seq")
    column = pl.ds(pl.multiple_of(s * mine, 128), mine)
    mine_o = tn(att_mine[0:half, :], branch_own[:, column]) + tn(att_mine[half:, :], branch_got[:, column])
    got_o = tn(att_got[half:, :], branch_own[:, column]) + tn(att_got[0:half, :], branch_got[:, column])
    start, stop, order = parts[with_o]
    to = slice(stop - start, stop - start + mine)
    for i in range(2):
        got = jnp.where(s == i, mine_o, got_o).astype(BF)
        for b in range(GROUPS // 2):
            place(
                got[b * rows : (b + 1) * rows, :], i * (GROUPS // 2) + b, order,
                outs[2 * with_o], outs[2 * with_o + 1], to,
            )


def pack_vectors(table, send, start):
    high = table.astype(BF)
    rest = (table - high.astype(F32)).astype(BF)
    width = min(table.shape[1], send.shape[1])
    row = start
    for piece in (high, rest):
        for c in range(0, table.shape[1], width):
            send[row : row + 16, 0:width] = piece[:, c : c + width]
            row += 16
    return high.astype(F32) + rest.astype(F32)


def unpack_vectors(got, start, total):
    width = min(total, got.shape[1])
    count = total // width
    parts = [got[start + 16 * i : start + 16 * (i + 1), 0:width].astype(F32) for i in range(2 * count)]
    return jnp.concatenate([parts[i] + parts[count + i] for i in range(count)], axis=1)


def vector_rows(total, cols):
    return 32 * (total // min(total, cols))


def grad_qkv_kernel(parts, with_vectors, own, other, grads, vec_f, vec_b, vec_a, *outs):
    half, width = own.shape
    mine = width // 2
    rows = width // GROUPS
    s = lax.axis_index("seq")
    for i in range(2):
        cols = slice(i * mine, (i + 1) * mine)
        for p, (start, stop, order) in enumerate(parts):
            for n in range(start, stop, mine):
                out = slice(n, n + mine)
                got = (
                    tn(own[:, cols], grads[0:half, out]) + tn(other[:, cols], grads[half:, out])
                ).astype(BF)
                to = slice(n - start, n - start + mine)
                for b in range(GROUPS // 2):
                    place(
                        got[b * rows : (b + 1) * rows, :], i * (GROUPS // 2) + b, order,
                        outs[2 * p], outs[2 * p + 1], to,
                    )
    zero = jnp.zeros((1, mine), F32)
    lines = []
    for r in range(2):
        line = vec_a[r : r + 1, :]
        lines.append(
            jnp.concatenate([jnp.where(s == 0, line, zero), jnp.where(s == 0, zero, line)], axis=1)
        )
    table = jnp.concatenate(lines + [vec_b[0:7, :], vec_f[0:3, :], jnp.zeros((4, width), F32)], axis=0)
    outs[-1][...] = pack_vectors(table, outs[2 * with_vectors + 1], GROUPS // 2 * rows)


def grad_input_kernel(grads, w_mine, sum1, pool, keep, send):
    half, width = sum1.shape
    mine = width // 2
    a, b = sum1[...], jnp.zeros((half, width), F32)
    for c in range(3):
        cols = slice(c * mine, (c + 1) * mine)
        a = a + nt(grads[0:half, cols], w_mine[c])
        b = b + nt(grads[half:, cols], w_mine[c])
    keep[...] = a
    send[0:half, :] = b
    send[half:, :] = pool[...]


def merge_kernel(rows, got, keep, keep_out, send_out):
    total = keep[0:rows, :].astype(F32) + got[0:rows, :].astype(F32)
    keep_out[...] = total[0 : rows // 2, :].astype(BF)
    send_out[...] = total[rows // 2 :, :].astype(BF)


def merge_vec_kernel(rows, got, keep, vec, keep_out, send_out, vec_out):
    merge_kernel(rows, got, keep, keep_out, send_out.at[0 : rows // 2, :])
    table = vec[...] + unpack_vectors(got, rows, vec.shape[1])
    vec_out[...] = pack_vectors(table, send_out, rows // 2)


def last_kernel(got, keep, keep_out, send_out, acc):
    rows = keep.shape[0]
    s = lax.axis_index("seq")
    acc[...] = keep[...].astype(F32) + got[0:rows, :].astype(F32)
    keep_out[...] = acc[pl.ds(pl.multiple_of(s * (rows // 2), 8), rows // 2), :]
    send_out[...] = acc[pl.ds(pl.multiple_of((1 - s) * (rows // 2), 8), rows // 2), :]


def last_vec_kernel(got, keep, vec, keep_out, send_out, acc):
    rows = keep.shape[0]
    last_kernel(got, keep, keep_out, send_out.at[0 : rows // 2, :], acc)
    table = vec[...] + unpack_vectors(got, rows, vec.shape[1])
    width = min(table.shape[1], keep.shape[1])
    for i, c in enumerate(range(0, table.shape[1], width)):
        send_out[rows // 2 + 16 * i : rows // 2 + 16 * (i + 1), 0:width] = table[:, c : c + width]


def finish_kernel(pieces, places, *refs):
    flat = refs[-1]
    count = len(places)
    per = count // pieces
    s = lax.axis_index("seq")
    for j, (p, lane) in enumerate(places):
        keep, got = refs[2 * p], refs[2 * p + 1]
        rows = keep.shape[0]
        cols = slice(lane, lane + 128)
        first, second = keep[:, cols], got[0:rows, cols]
        line = j // per * 2 * per + j % per
        flat[pl.ds(line, rows, stride=2 * count), :] = jnp.where(s == 0, first, second)
        flat[pl.ds(line + per, rows, stride=2 * count), :] = jnp.where(s == 0, second, first)


def finish_vectors_kernel(rows, width, sent, got, b_qv, b_o, gain1, shift1, b_in, b_out, gain2, shift2):
    half = min(width, sent.shape[1])
    count = width // half
    total = sent[rows:, 0:half] + got[rows:, 0:half]
    table = jnp.concatenate([total[16 * i : 16 * (i + 1), :] for i in range(count)], axis=1)
    b_qv[...] = table[0:2, :]
    base = b_in.shape[0] * 128 // width
    for r in range(base):
        for c in range(width // 128):
            line = r * (width // 128) + c
            b_in[line : line + 1, :] = table[2 + r : 3 + r, c * 128 : (c + 1) * 128]
    for i, ref in enumerate((gain1, shift1, b_o, gain2, shift2, b_out)):
        for c in range(width // 128):
            ref[c : c + 1, :] = table[2 + base + i : 3 + base + i, c * 128 : (c + 1) * 128]


def finish_input_kernel(lens, keep, sent, got, d_input, pooled):
    half = keep.shape[0]
    d_input[...] = keep[...] + got[0:half, :]
    total = sent[half:, :] + got[half:, :]
    for t in range(lens.shape[1]):
        pooled[t : t + 1, :] = total[t : t + 1, :] / lens[0, t].astype(F32)


def swap(x, axis="seq"):
    return lax.ppermute(x, axis, [(0, 1), (1, 0)])


def send_to(x, phase, order, count):
    pairs = []
    for d in range(count):
        for s in range(2):
            pairs.append((2 * d + s, 2 * (d ^ (1 << order[s][phase])) + s))
    return lax.ppermute(x, ("dp", "seq"), pairs)


class Part:
    def __init__(self, keep, send, order, vec):
        self.keep, self.sent, self.order, self.vec, self.got = keep, send, order, vec, None


class Sum:
    def __init__(self, line, parts, count, name):
        self.line, self.parts, self.count, self.name = line, parts, count, name
        self.phase = 0
        self.send()

    def send(self):
        for part in self.parts:
            if self.phase == len(part.order[0]):
                part.got = swap(part.sent)
            else:
                part.got = send_to(part.sent, self.phase, part.order, self.count)

    def step(self):
        last = self.phase == len(self.parts[0].order[0]) - 1
        dtype = F32 if last else BF
        args, outs, scratch, jobs = [], [], [], []
        for part in self.parts:
            rows, cols = part.keep.shape
            half = rows // 2
            extra = 0 if part.vec is None else vector_rows(part.vec.shape[1], cols)
            args += [part.got, part.keep]
            outs += [sds((half, cols), dtype), sds((half + (extra // 2 if last else extra), cols), dtype)]
            if last:
                scratch.append(pltpu.VMEM((rows, cols), F32))
            if part.vec is None:
                jobs.append((last_kernel if last else functools.partial(merge_kernel, rows), 2, 2))
            elif last:
                args.append(part.vec)
                jobs.append((last_vec_kernel, 3, 2))
            else:
                args.append(part.vec)
                outs.append(sds(part.vec.shape, F32))
                jobs.append((functools.partial(merge_vec_kernel, rows), 3, 3))

        def kernel(*refs):
            i, o, t = 0, len(args), len(args) + len(outs)
            for run, reads, writes in jobs:
                run(*refs[i : i + reads], *refs[o : o + writes], *([refs[t]] if last else []))
                i, o, t = i + reads, o + writes, t + 1

        made = self.line.call(
            kernel, outs, *args, scratch=scratch, name=f"sum_{self.name}_{self.phase}", vmem=10, us=MERGE_US
        )
        made = list(made)
        for part, (_, _, writes) in zip(self.parts, jobs):
            part.keep, part.sent = made[0], made[1]
            if writes == 3:
                part.vec = made[2]
            del made[:writes]
        self.phase += 1
        self.send()


def interleave(keep, got, s, pieces):
    size = keep.shape[1] // pieces
    outs = []
    for i in range(pieces):
        a, b = keep[:, i * size : (i + 1) * size], got[:, i * size : (i + 1) * size]
        outs += [jnp.where(s == 0, a, b), jnp.where(s == 0, b, a)]
    return outs


def on_device(
    spread, count,
    hidden_in, w_qkv, b_qv, w_o, b_o, ln1_gain, ln1_bias, w_in, b_in, w_out, b_out, ln2_gain, ln2_bias,
    seg_lengths, cotangent,
):
    row_count, half, width = hidden_in.shape
    length = 2 * half
    mine = width // 2
    heads = HEADS // 2
    ff = w_in.shape[1]
    s = lax.axis_index("seq")
    own = hidden_in.reshape(half, width)
    cot = cotangent.reshape(half, width)
    line = Line()
    call = line.call
    flat = lambda x: x.reshape(1, -1)
    rows_ff, rows_w = ff // GROUPS, width // GROUPS
    half_ff, half_w = GROUPS // 2 * rows_ff, GROUPS // 2 * rows_w
    made, sums, flats = {}, {}, {}

    def parts_of(weight):
        names = [n for n in PARTS if PARTS[n][0] == weight]
        return names, tuple(
            (PARTS[n][1], PARTS[n][2], both_cores(PARTS[n][3]) if spread else None) for n in names
        )

    def reduce(names, arrays):
        for i, name in enumerate(names):
            keep, send = arrays[2 * i], arrays[2 * i + 1]
            vec = made["table"] if name == WITH_VECTORS else None
            sums[name] = Part(keep, send, both_cores(PARTS[name][3]), vec)
        if spread:
            weight = PARTS[names[0]][0]
            sums[weight] = Sum(line, [sums[n] for n in names], count, weight)

    other = swap(own)
    own, w_mine, bias, lin = call(
        project_kernel,
        [sds((half, width), BF), sds((3, width, mine), BF), sds((8, mine), F32), sds((half, 3 * mine), F32)],
        own, w_qkv, b_qv,
        hbm=(0, 1, 2), scratch=[pltpu.VMEM(b_qv.shape, BF), pltpu.SemaphoreType.DMA((5,))],
        name="project", vmem=12,
    )
    q, k, v, kt, expo, scale, att_t, att_mine, w_o, w_in, w_out = call(
        attend_kernel,
        [sds((length, mine), BF)] * 3
        + [sds((mine, length), BF), sds((heads, length, length), BF), sds((8, length), F32)]
        + [sds((mine, length), F32), sds((length, mine), BF)]
        + [sds(w.shape, BF) for w in (w_o, w_in, w_out)],
        seg_lengths, other, w_mine, bias, lin, w_o, w_in, w_out,
        smem=(0,), hbm=(5, 6, 7), scratch=[pltpu.SemaphoreType.DMA((3,))], name="attend", vmem=16,
    )
    att_got = swap(att_mine)
    (mid_low, active, pull, normal, inverse, sum2, down_own, down_send, output, pool_part, vec_f) = call(
        forward_kernel,
        [
            sds((half, width), BF), sds((half, ff), BF), sds((half, ff), F32), sds((half, width), F32),
            sds((half, 1), F32), sds((half, width), F32), sds((half, mine), BF), sds((half, mine), BF),
            sds((half, width), BF), sds((8, width), F32), sds((8, width), F32),
        ],
        seg_lengths, own, att_mine, att_got, w_o, flat(b_o), flat(ln1_gain), flat(ln1_bias), w_in, flat(b_in),
        w_out, flat(b_out), flat(ln2_gain), flat(ln2_bias), cot,
        smem=(0,), scratch=[pltpu.VMEM((half, width), F32)], name="forward", vmem=16,
    )
    active_got = swap(active)
    mid_got = swap(mid_low)
    down_got = swap(down_send)

    def backward():
        made["up_own"], up_send, made["sum1"], branch, made["vec_b"] = call(
            backward_kernel,
            [
                sds((half, ff // 2), BF), sds((half, ff // 2), BF), sds((half, width), F32),
                sds((half, width), BF), sds((8, width), F32),
            ],
            sum2, pull, normal, inverse, flat(ln1_gain), w_in, w_out,
            scratch=[pltpu.VMEM((half, width), F32)], name="backward", vmem=12,
        )
        made["branch"] = branch, swap(branch)
        made["up_got"] = swap(up_send)

    def grad_out():
        names, parts = parts_of("out")
        outs = [sds((half_ff, stop - start), BF) for start, stop, _ in parts for _ in range(2)]
        arrays = call(
            functools.partial(grad_out_kernel, parts), outs,
            active, active_got, down_own, down_got, name="grad_out",
        )
        reduce(names, arrays)

    def grad_in():
        names, parts = parts_of("in")
        with_o = names.index(WITH_O)
        outs = []
        for i, (start, stop, _) in enumerate(parts):
            outs += [sds((half_w, stop - start + (mine if i == with_o else 0)), BF)] * 2
        arrays = call(
            functools.partial(grad_in_kernel, parts, with_o), outs,
            mid_low, mid_got, made["up_own"], made["up_got"], att_mine, att_got, *made["branch"], name="grad_in",
        )
        reduce(names, arrays)

    def attend_back():
        made["grads"], made["vec_a"] = call(
            attend_back_kernel, [sds((length, 3 * mine), BF), sds((8, mine), F32)],
            *made["branch"], w_o, q, k, v, kt, expo, scale, att_t, name="attend_back", vmem=16,
        )

    def grad_qkv():
        names, parts = parts_of("qkv")
        with_vectors = names.index(WITH_VECTORS)
        outs = []
        for i, (start, stop, _) in enumerate(parts):
            extra = vector_rows(width, stop - start) if i == with_vectors else 0
            outs += [sds((half_w, stop - start), BF), sds((half_w + extra, stop - start), BF)]
        outs.append(sds((16, width), F32))
        *arrays, made["table"] = call(
            functools.partial(grad_qkv_kernel, parts, with_vectors), outs,
            own, other, made["grads"], vec_f, made["vec_b"], made["vec_a"], name="grad_qkv",
        )
        reduce(names, arrays)

    def grad_input():
        made["keep"], made["send"] = call(
            grad_input_kernel, [sds((half, width), F32), sds((half + 8, width), F32)],
            made["grads"], w_mine, made["sum1"], pool_part, name="grad_input",
        )
        made["got"] = swap(made["send"])

    def finish_input():
        made["d_input"], made["pooled"] = call(
            finish_input_kernel, [sds((half, width), F32), sds((seg_lengths.shape[1], width), F32)],
            seg_lengths, made["keep"], made["send"], made["got"], smem=(0,), name="finish_input", end=True,
        )

    def places_of(weight, pieces):
        if weight == "o":
            _, start, stop, _ = PARTS[WITH_O]
            return [WITH_O], [(0, stop - start + c) for c in range(0, mine, 128)]
        names, parts = parts_of(weight)
        return names, [
            (i, c - start) for i, (start, stop, _) in enumerate(parts) for c in range(start, stop, 128)
        ]

    def finish_all():
        args, outs, jobs = [], [], []
        for weight, pieces in WEIGHTS.items():
            names, places = places_of(weight, pieces)
            first = len(args)
            args += [x for n in names for x in (sums[n].keep, sums[n].got)]
            outs.append(sds((2 * args[first].shape[0] * len(places), 128), F32))
            jobs.append((functools.partial(finish_kernel, pieces, places), first, len(args)))
        part = sums[WITH_VECTORS]
        one = sds((width // 128, 128), F32)
        args += [part.sent, part.got]
        outs += [sds((2, width), F32), one, one, one, sds((ff // 128, 128), F32), one, one, one]

        def kernel(*refs):
            results = refs[len(args) :]
            for job, (run, start, stop) in enumerate(jobs):
                run(*refs[start:stop], results[job])
            finish_vectors_kernel(
                part.keep.shape[0], width, refs[len(args) - 2], refs[len(args) - 1], *results[len(jobs) :]
            )

        done = call(kernel, outs, *args, name="finish", vmem=10)
        for weight, out in zip(WEIGHTS, done):
            flats[weight] = out.reshape(-1)
        made["vectors"] = done[len(jobs) :]

    work = {
        "BWD": backward, "OUT": grad_out, "IN": grad_in, "BACK": attend_back, "QKV": grad_qkv, "INPUT": grad_input,
        "input": finish_input,
    }
    for item in PLAN:
        if item in work:
            work[item]()
        elif spread:
            sums[item].step()
    if spread:
        finish_all()

    if spread:
        vectors = [v if v.shape[0] == 2 else v.reshape(-1) for v in made["vectors"]]
    else:
        for name in PARTS:
            part = sums[name]
            both = jnp.concatenate([part.keep, part.sent[: part.keep.shape[0]]], axis=0)
            total = lax.psum_scatter(both, "dp", scatter_dimension=0, tiled=True).astype(F32)
            half_rows = total.reshape(2, -1, total.shape[1])
            part.keep = jnp.where(s == 0, half_rows[0], half_rows[1])
            part.got = swap(jnp.where(s == 0, half_rows[1], half_rows[0]))
        for weight, pieces in WEIGHTS.items():
            names, places = places_of(weight, pieces)
            keep, got = (
                jnp.concatenate([getattr(sums[names[p]], k)[:, c : c + 128] for p, c in places], axis=1)
                for k in ("keep", "got")
            )
            flats[weight] = jnp.concatenate(interleave(keep, got, s, pieces), axis=1).reshape(-1)
        vec = lax.psum(made["table"], ("dp", "seq"))
        base = ff // width
        vectors = [vec[0:2]] + [vec[2 + base + i] for i in (2, 0, 1)] + [vec[2 : 2 + base].reshape(-1)]
        vectors += [vec[2 + base + i] for i in (5, 3, 4)]
    return (
        output.reshape(row_count, half, width),
        made["pooled"][None],
        made["d_input"].reshape(row_count, half, width),
        *(flats[n] for n in ("qkv", "o", "in", "out")),
        *vectors,
    )


def both_cores(letters):
    bits = {"x": 0, "y": 1, "1": 2, "2": 3}
    turned = {"x": "y", "y": "x"}
    return tuple(bits[c] for c in letters), tuple(bits[turned.get(c, c)] for c in letters)


def solution(mesh):
    count = mesh.shape["dp"]
    in_specs = (P("dp", "seq", None),) + (P(),) * 12 + (P("dp", None), P("dp", "seq", None))
    out_specs = (
        P("dp", "seq", None),
        P("dp", None, None),
        P("dp", "seq", None),
    ) + (P(("dp", "seq")),) * 4 + (P(),) * 8
    return jax.shard_map(
        functools.partial(on_device, count == GROUPS, count),
        mesh=mesh, in_specs=in_specs, out_specs=out_specs, check_vma=False,
    )
```

```python
import functools
import math

import jax
import jax.numpy as jnp
from jax import lax
from jax.experimental import pallas as pl
from jax.experimental.pallas import tpu as pltpu
from jax.sharding import PartitionSpec as P

HEADS = 12
EPSILON = 1e-12
HIDE = -1e30
GROUPS = 16
BF = jnp.bfloat16
F32 = jnp.float32
MIB = 2**20
PIECES = 1
MERGE_US = 1.0
KERNEL_US = 1.0
WEIGHTS = {"out": 1, "in": 1, "qkv": 3, "o": 1}
PARTS = {
    "a": ("out", 0, 384, "y1x2", "12xy"),
    "b": ("in", 0, 1024, "y1x2", "xy12"),
    "c": ("in", 1024, 1536, "1yx2", "yx21"),
    "d": ("qkv", 0, 1152, "x2y1", "xy12"),
}
WITH_O = "c"
WITH_VECTORS = "d"
PLAN = (
    "BWD", "OUT", "BACK", "QKV", "IN", "INPUT", "out", "qkv", "in", "input", "out", "qkv",
    "in", "out", "qkv", "in", "out", "qkv", "in",
)


def sds(shape, dtype):
    return jax.ShapeDtypeStruct(shape, dtype)


def nn(left, right):
    return jnp.dot(left, right, preferred_element_type=F32)


def nt(left, right):
    return lax.dot_general(left, right, (((1,), (1,)), ((), ())), preferred_element_type=F32)


def tn(left, right):
    return lax.dot_general(left, right, (((0,), (0,)), ((), ())), preferred_element_type=F32)


class Line:
    def __init__(self):
        self.last = None

    def call(self, kernel, outs, *args, scratch=(), hbm=(), smem=(), name=None, vmem=16, us=KERNEL_US, end=False):
        if end:
            outs = [sds((8, 128), F32), *outs]
        specs = []
        lead = len(args)
        for i in range(lead):
            space = pltpu.HBM if i in hbm else pltpu.SMEM if i in smem else pltpu.VMEM
            specs.append(pl.BlockSpec(memory_space=space))
        args = [
            pltpu.with_memory_space_constraint(arg, pltpu.HBM) if i in hbm else arg
            for i, arg in enumerate(args)
        ]
        after = () if self.last is None else (self.last,)
        specs += [pl.BlockSpec(memory_space=pl.ANY) for _ in after]

        def body(*refs):
            rest = refs[lead + len(after) :]
            if end:
                rest[0][...] = jnp.zeros((8, 128), F32)
                rest = rest[1:]
            kernel(*refs[:lead], *rest)

        made = pl.pallas_call(
            body,
            out_shape=list(outs),
            in_specs=specs,
            out_specs=[pl.BlockSpec(memory_space=pltpu.VMEM) for _ in outs],
            scratch_shapes=list(scratch),
            compiler_params=pltpu.CompilerParams(vmem_limit_bytes=vmem * MIB),
            cost_estimate=pl.CostEstimate(flops=int(us * 1.1e9), bytes_accessed=1024, transcendentals=0),
            name=name,
        )(*args, *after)
        self.last = made[0]
        return made[1:] if end else made


def segment_of(positions, lens_ref):
    ids = jnp.zeros_like(positions)
    end = jnp.int32(0)
    for j in range(lens_ref.shape[1]):
        end = end + lens_ref[0, j]
        ids = ids + (positions >= end).astype(jnp.int32)
    return ids


def own_first(index, half, s):
    return jnp.where(index < half, index + s * half, index - half + (1 - s) * half)


def normalise(total):
    centered = total - jnp.mean(total, axis=-1, keepdims=True)
    inverse = lax.rsqrt(jnp.mean(centered * centered, axis=-1, keepdims=True) + EPSILON)
    return centered * inverse, inverse


def norm_pull(grad, normal, inverse, gain):
    scaled = grad * gain
    return inverse * (
        scaled
        - jnp.mean(scaled, axis=-1, keepdims=True)
        - normal * jnp.mean(scaled * normal, axis=-1, keepdims=True)
    )


def column_sum(matrix):
    return jnp.sum(matrix, axis=0, keepdims=True)


def copies_of(source, target, sems, first, pieces):
    rows = target.shape[0] // pieces
    return [
        pltpu.make_async_copy(
            source.at[i * rows : (i + 1) * rows, :], target.at[i * rows : (i + 1) * rows, :], sems.at[first + i]
        )
        for i in range(pieces)
    ]


def project_kernel(own_hbm, w_hbm, b_hbm, own, w_mine, bias, lin, b_buf, sems):
    width = own.shape[1]
    mine = width // 2
    s = lax.axis_index("seq")
    first = pltpu.make_async_copy(own_hbm, own, sems.at[3 * PIECES])
    first.start()
    copies = []
    for c in range(3):
        start = pl.multiple_of(c * width + s * mine, 128)
        copies.append(copies_of(w_hbm.at[:, pl.ds(start, mine)], w_mine.at[c], sems, c * PIECES, PIECES))
        for copy in copies[-1]:
            copy.start()
    second = pltpu.make_async_copy(b_hbm, b_buf, sems.at[3 * PIECES + 1])
    second.start()
    second.wait()
    column = pl.ds(pl.multiple_of(s * mine, 128), mine)
    bias[...] = jnp.zeros_like(bias)
    bias[0:1, :] = b_buf[0:1, column].astype(F32)
    bias[2:3, :] = b_buf[1:2, column].astype(F32)
    first.wait()
    for c in range(3):
        for copy in copies[c]:
            copy.wait()
        lin[:, c * mine : (c + 1) * mine] = nn(own[...], w_mine[c]) + bias[c : c + 1, :]


def attend_kernel(
    lens, other, w_mine, bias, lin, w_o_hbm, w_in_hbm, w_out_hbm,
    q_out, k_out, v_out, kt_out, expo_out, scale_out, att_t, att_out, w_o, w_in, w_out, sems,
):
    half, width = other.shape
    length = 2 * half
    mine = width // 2
    pair = 2 * (width // HEADS)
    head = pair // 2
    s = lax.axis_index("seq")
    copies = []
    for source, target in ((w_o_hbm, w_o), (w_in_hbm, w_in), (w_out_hbm, w_out)):
        copies += copies_of(source, target, sems, len(copies), PIECES)
    for copy in copies:
        copy.start()
    parts = []
    for c in range(3):
        rest = nn(other[...], w_mine[c]) + bias[c : c + 1, :]
        parts.append(jnp.concatenate([lin[:, c * mine : (c + 1) * mine], rest], axis=0))
    q_all, k_all, v_all = parts
    q_all = q_all.astype(BF).astype(F32) * (1.0 / math.sqrt(head))
    q_out[...] = q_all.astype(BF)
    k_out[...] = k_all.astype(BF)
    v_out[...] = v_all.astype(BF)
    kt_out[...] = k_all.T.astype(BF)
    vt = v_all.T.astype(BF)
    rows = own_first(lax.broadcasted_iota(jnp.int32, (length, pair), 0), half, s)
    lane = lax.broadcasted_iota(jnp.int32, (length, pair), 1)
    same = segment_of(rows, lens) == lane % head
    in_range = lane % head < lens.shape[1]
    mark_k = jnp.where(same, 1.0, 0.0)
    mark_q = jnp.where(jnp.logical_and(in_range, jnp.logical_not(same)), HIDE, 0.0)
    first = lane < head
    for j in range(mine // pair):
        cols = slice(j * pair, (j + 1) * pair)
        q2, k2 = q_all[:, cols], k_all[:, cols]
        pieces = []
        for a in range(2):
            keep = first if a == 0 else jnp.logical_not(first)
            k_m = jnp.where(keep, k2, mark_k).astype(BF)
            q_m = jnp.where(keep, q2, mark_q).astype(BF)
            scores = nt(k_m, q_m)
            top = jnp.max(scores, axis=0, keepdims=True)
            expo = jnp.exp(scores - top)
            scale = 1.0 / jnp.sum(expo, axis=0, keepdims=True)
            low = expo.astype(BF)
            h = 2 * j + a
            expo_out[h] = low
            scale_out[h : h + 1, :] = scale
            pieces.append(nn(vt[h * head : (h + 1) * head, :], low) * scale)
        both = jnp.concatenate(pieces, axis=0)
        att_t[cols, :] = both
        att_out[:, cols] = both.T.astype(BF)
    for copy in copies:
        copy.wait()


def forward_kernel(
    lens,
    own,
    att_mine,
    att_got,
    w_o,
    b_o,
    gain1,
    shift1,
    w_in,
    b_in,
    w_out,
    b_out,
    gain2,
    shift2,
    cot,
    mid_out,
    active_out,
    pull_out,
    normal_out,
    inverse_out,
    sum2_out,
    down_keep,
    down_send,
    out_out,
    pool_out,
    vec_out,
    down_acc,
):
    half, width = own.shape
    mine = width // 2
    ff = w_in.shape[1]
    s = lax.axis_index("seq")
    row_a = pl.ds(pl.multiple_of(s * mine, 128), mine)
    row_b = pl.ds(pl.multiple_of((1 - s) * mine, 128), mine)
    branch = nn(att_mine[0:half, :], w_o[row_a, :]) + nn(att_got[half:, :], w_o[row_b, :])
    normal, inverse = normalise(own[...].astype(F32) + (branch + b_o[...].astype(F32)))
    middle = normal * gain1[...].astype(F32) + shift1[...].astype(F32)
    low = middle.astype(BF)
    mid_out[...] = low
    normal_out[...] = normal
    inverse_out[...] = inverse
    down_acc[...] = middle + b_out[...].astype(F32)
    step = 1024
    for c in range(0, ff, step):
        cols = slice(c, c + step)
        upper = nn(low, w_in[:, cols]) + b_in[:, cols].astype(F32)
        cdf = 0.5 + 0.5 * lax.erf(upper * (1.0 / math.sqrt(2.0)))
        density = jnp.exp(-0.5 * upper * upper) * (1.0 / math.sqrt(2.0 * math.pi))
        act = (upper * cdf).astype(BF)
        active_out[:, cols] = act
        pull_out[:, cols] = cdf + upper * density
        down_acc[...] += nn(act, w_out[cols, :])
    normal2, inverse2 = normalise(down_acc[...])
    gain = gain2[...].astype(F32)
    final = normal2 * gain + shift2[...].astype(F32)
    out_out[...] = final.astype(BF)
    rows = lax.broadcasted_iota(jnp.int32, (half, width), 0) + s * half
    ids = segment_of(rows, lens)
    pool_out[...] = jnp.zeros_like(pool_out)
    for t in range(lens.shape[1]):
        pool_out[t : t + 1, :] = column_sum(jnp.where(ids == t, final, 0.0))
    grad = cot[...].astype(F32)
    sum2 = norm_pull(grad, normal2, inverse2, gain)
    sum2_out[...] = sum2
    down = sum2.astype(BF)
    down_acc[...] = sum2
    down_keep[...] = down_acc[:, row_a].astype(BF)
    down_send[...] = down_acc[:, row_b].astype(BF)
    vec_out[...] = jnp.zeros_like(vec_out)
    vec_out[0:1, :] = column_sum(grad * normal2)
    vec_out[1:2, :] = column_sum(grad)
    vec_out[2:3, :] = column_sum(down.astype(F32))


def backward_kernel(
    sum2, pull, normal, inverse, gain1, w_in, w_out,
    up_keep, up_send, sum1_out, branch_out, vec_out, mid_acc,
):
    width, ff = w_in.shape
    s = lax.axis_index("seq")
    step = 768
    per = ff // 2 // step
    mid_acc[...] = sum2[...]
    low = sum2[...].astype(BF)
    vec_out[...] = jnp.zeros_like(vec_out)
    sums = []
    for i in range(2 * per):
        block = (i // per + s) % 2
        start = pl.multiple_of(block * (ff // 2) + (i % per) * step, 128)
        cols = pl.ds(start, step)
        grad_upper = (nt(low, w_out[cols, :]) * pull[:, cols]).astype(BF)
        place = up_keep if i < per else up_send
        place[:, (i % per) * step : (i % per + 1) * step] = grad_upper
        sums.append(column_sum(grad_upper.astype(F32)))
        mid_acc[...] += nt(grad_upper, w_in[:, cols])
    ups = [jnp.concatenate(sums[:per], axis=1), jnp.concatenate(sums[per:], axis=1)]
    for b in range(2):
        line = jnp.where(s == b, ups[0], ups[1])
        for r in range(ff // 2 // width):
            row = b * (ff // 2 // width) + r
            vec_out[row : row + 1, :] = line[:, r * width : (r + 1) * width]
    base = ff // width
    grad_mid = mid_acc[...]
    vec_out[base : base + 1, :] = column_sum(grad_mid * normal[...])
    vec_out[base + 1 : base + 2, :] = column_sum(grad_mid)
    sum1 = norm_pull(grad_mid, normal[...], inverse[...], gain1[...].astype(F32))
    sum1_out[...] = sum1
    branch = sum1.astype(BF)
    branch_out[...] = branch
    vec_out[base + 2 : base + 3, :] = column_sum(branch.astype(F32))


def attend_back_kernel(
    branch_own, branch_got, w_o, q, k, v, kt, expo, scale, att_t, grad_out, vec_out
):
    length, mine = q.shape
    width = w_o.shape[1]
    head = width // HEADS
    pair = 2 * head
    s = lax.axis_index("seq")
    w_mine = w_o[pl.ds(pl.multiple_of(s * mine, 128), mine), :]
    grad_t = jnp.concatenate([nt(w_mine, branch_own[...]), nt(w_mine, branch_got[...])], axis=1)
    lane = lax.broadcasted_iota(jnp.int32, (length, pair), 1)
    first = lane < head
    vec_out[...] = jnp.zeros_like(vec_out)
    for j in range(mine // pair):
        cols = slice(j * pair, (j + 1) * pair)
        q2 = q[:, cols]
        v2 = v[:, cols].astype(F32)
        scaled, inners = [], []
        for h in (2 * j, 2 * j + 1):
            part = slice(h * head, (h + 1) * head)
            times = scale[h : h + 1, :]
            scaled.append(grad_t[part, :] * times)
            inners.append(jnp.sum(att_t[part, :] * scaled[-1], axis=0, keepdims=True))
        a2 = jnp.concatenate(scaled, axis=0).astype(BF)
        dq, dk, dv = [], [], []
        for a in range(2):
            h = 2 * j + a
            keep = first if a == 0 else jnp.logical_not(first)
            v_m = jnp.where(keep, v2, 0.0).astype(BF)
            grad_p = nn(v_m, a2)
            low = expo[h]
            raw = (low.astype(F32) * (grad_p - inners[a])).astype(BF)
            dk.append(nn(raw, q2))
            dv.append(nt(low, a2))
            dq.append(nn(kt[h * head : (h + 1) * head, :], raw))
        dq_low = (jnp.concatenate(dq, axis=0) * (1.0 / math.sqrt(head))).astype(BF).T
        dk_low = jnp.where(first, dk[0], dk[1]).astype(BF)
        dv_low = jnp.where(first, dv[0], dv[1]).astype(BF)
        grad_out[:, cols] = dq_low
        grad_out[:, mine + j * pair : mine + (j + 1) * pair] = dk_low
        grad_out[:, 2 * mine + j * pair : 2 * mine + (j + 1) * pair] = dv_low
        vec_out[0:1, cols] = column_sum(dq_low.astype(F32))
        vec_out[1:2, cols] = column_sum(dv_low.astype(F32))


def chunk_of(slot, order):
    if order is None:
        return slot
    chunks = []
    for bits in order:
        rel = 0
        for i, bit in enumerate(bits):
            rel |= (slot >> (len(bits) - 1 - i) & 1) << bit
        chunks.append(rel)
    rel = jnp.where(lax.axis_index("seq") == 0, jnp.int32(chunks[0]), jnp.int32(chunks[1]))
    return jnp.bitwise_xor(rel, lax.axis_index("dp"))


def spread_rows(whole, order, keep, send, cols, to):
    rows = whole.shape[0] // GROUPS
    for slot in range(GROUPS):
        chunk = chunk_of(slot, order)
        target = keep if slot < GROUPS // 2 else send
        place = slot % (GROUPS // 2) * rows
        target[place : place + rows, to] = whole[pl.ds(pl.multiple_of(chunk * rows, 16), rows), cols]


def grad_out_kernel(parts, active_own, active_got, down_own, down_got, *outs):
    *outs, whole = outs
    block = 512
    for i in range(0, active_own.shape[1], block):
        cols = slice(i, i + block)
        whole[cols, :] = (
            tn(active_own[:, cols], down_own[...]) + tn(active_got[:, cols], down_got[...])
        ).astype(BF)
    for p, (start, stop, order) in enumerate(parts):
        spread_rows(whole, order, outs[2 * p], outs[2 * p + 1], slice(start, stop), slice(0, stop - start))


def grad_in_kernel(
    parts, with_o, mid_own, mid_got, up_own, up_got, att_mine, att_got, branch_own, branch_got, *outs
):
    *outs, whole, whole_o = outs
    half, width = mid_own.shape
    mine = width // 2
    for i in range(2):
        cols = slice(i * mine, (i + 1) * mine)
        own_t, got_t = mid_own[:, cols].T, mid_got[:, cols].T
        for n in range(0, up_own.shape[1], 512):
            out = slice(n, n + 512)
            whole[cols, out] = (nn(own_t, up_own[:, out]) + nn(got_t, up_got[:, out])).astype(BF)
    s = lax.axis_index("seq")
    column = pl.ds(pl.multiple_of(s * mine, 128), mine)
    mine_o = tn(att_mine[0:half, :], branch_own[:, column]) + tn(att_mine[half:, :], branch_got[:, column])
    got_o = tn(att_got[half:, :], branch_own[:, column]) + tn(att_got[0:half, :], branch_got[:, column])
    for i in range(2):
        whole_o[i * mine : (i + 1) * mine, :] = jnp.where(s == i, mine_o, got_o).astype(BF)
    for p, (start, stop, order) in enumerate(parts):
        spread_rows(whole, order, outs[2 * p], outs[2 * p + 1], slice(start, stop), slice(0, stop - start))
        if p == with_o:
            to = slice(stop - start, stop - start + mine)
            spread_rows(whole_o, order, outs[2 * p], outs[2 * p + 1], slice(0, mine), to)


def pack_vectors(table, send, start):
    high = table.astype(BF)
    rest = (table - high.astype(F32)).astype(BF)
    width = min(table.shape[1], send.shape[1])
    row = start
    for piece in (high, rest):
        for c in range(0, table.shape[1], width):
            send[row : row + 16, 0:width] = piece[:, c : c + width]
            row += 16
    return high.astype(F32) + rest.astype(F32)


def unpack_vectors(got, start, total):
    width = min(total, got.shape[1])
    count = total // width
    parts = [got[start + 16 * i : start + 16 * (i + 1), 0:width].astype(F32) for i in range(2 * count)]
    return jnp.concatenate([parts[i] + parts[count + i] for i in range(count)], axis=1)


def vector_rows(total, cols):
    return 32 * (total // min(total, cols))


def grad_qkv_kernel(parts, with_vectors, own, other, grads, vec_f, vec_b, vec_a, *outs):
    *outs, whole = outs
    half, width = own.shape
    mine = width // 2
    rows = width // GROUPS
    s = lax.axis_index("seq")
    for i in range(2):
        cols = slice(i * mine, (i + 1) * mine)
        both_t = jnp.concatenate([own[:, cols].T, other[:, cols].T], axis=1)
        for c in range(3):
            out = slice(c * mine, (c + 1) * mine)
            whole[cols, out] = nn(both_t, grads[:, out]).astype(BF)
    for p, (start, stop, order) in enumerate(parts):
        spread_rows(whole, order, outs[2 * p], outs[2 * p + 1], slice(start, stop), slice(0, stop - start))
    zero = jnp.zeros((1, mine), F32)
    lines = []
    for r in range(2):
        line = vec_a[r : r + 1, :]
        lines.append(
            jnp.concatenate([jnp.where(s == 0, line, zero), jnp.where(s == 0, zero, line)], axis=1)
        )
    table = jnp.concatenate(lines + [vec_b[0:7, :], vec_f[0:3, :], jnp.zeros((4, width), F32)], axis=0)
    outs[-1][...] = pack_vectors(table, outs[2 * with_vectors + 1], GROUPS // 2 * rows)


def grad_input_kernel(grads, w_mine, sum1, pool, keep, send):
    half, width = sum1.shape
    mine = width // 2
    a, b = sum1[...], jnp.zeros((half, width), F32)
    for c in range(3):
        cols = slice(c * mine, (c + 1) * mine)
        a = a + nt(grads[0:half, cols], w_mine[c])
        b = b + nt(grads[half:, cols], w_mine[c])
    keep[...] = a
    send[0:half, :] = b
    send[half:, :] = pool[...]


def merge_kernel(rows, got, keep, keep_out, send_out):
    total = keep[0:rows, :].astype(F32) + got[0:rows, :].astype(F32)
    keep_out[...] = total[0 : rows // 2, :].astype(BF)
    send_out[...] = total[rows // 2 :, :].astype(BF)


def merge_vec_kernel(rows, got, keep, vec, keep_out, send_out, vec_out):
    merge_kernel(rows, got, keep, keep_out, send_out.at[0 : rows // 2, :])
    table = vec[...] + unpack_vectors(got, rows, vec.shape[1])
    vec_out[...] = pack_vectors(table, send_out, rows // 2)


def last_kernel(got, keep, keep_out, send_out, acc):
    rows = keep.shape[0]
    s = lax.axis_index("seq")
    acc[...] = keep[...].astype(F32) + got[0:rows, :].astype(F32)
    keep_out[...] = acc[pl.ds(pl.multiple_of(s * (rows // 2), 8), rows // 2), :]
    send_out[...] = acc[pl.ds(pl.multiple_of((1 - s) * (rows // 2), 8), rows // 2), :]


def last_vec_kernel(got, keep, vec, keep_out, send_out, acc):
    rows = keep.shape[0]
    last_kernel(got, keep, keep_out, send_out.at[0 : rows // 2, :], acc)
    table = vec[...] + unpack_vectors(got, rows, vec.shape[1])
    width = min(table.shape[1], keep.shape[1])
    for i, c in enumerate(range(0, table.shape[1], width)):
        send_out[rows // 2 + 16 * i : rows // 2 + 16 * (i + 1), 0:width] = table[:, c : c + width]


def finish_kernel(pieces, places, *refs):
    flat = refs[-1]
    count = len(places)
    per = count // pieces
    s = lax.axis_index("seq")
    for j, (p, lane) in enumerate(places):
        keep, got = refs[2 * p], refs[2 * p + 1]
        rows = keep.shape[0]
        cols = slice(lane, lane + 128)
        first, second = keep[:, cols], got[0:rows, cols]
        line = j // per * 2 * per + j % per
        flat[pl.ds(line, rows, stride=2 * count), :] = jnp.where(s == 0, first, second)
        flat[pl.ds(line + per, rows, stride=2 * count), :] = jnp.where(s == 0, second, first)


def finish_vectors_kernel(rows, width, sent, got, b_qv, b_o, gain1, shift1, b_in, b_out, gain2, shift2):
    half = min(width, sent.shape[1])
    count = width // half
    total = sent[rows:, 0:half] + got[rows:, 0:half]
    table = jnp.concatenate([total[16 * i : 16 * (i + 1), :] for i in range(count)], axis=1)
    b_qv[...] = table[0:2, :]
    base = b_in.shape[0] * 128 // width
    for r in range(base):
        for c in range(width // 128):
            line = r * (width // 128) + c
            b_in[line : line + 1, :] = table[2 + r : 3 + r, c * 128 : (c + 1) * 128]
    for i, ref in enumerate((gain1, shift1, b_o, gain2, shift2, b_out)):
        for c in range(width // 128):
            ref[c : c + 1, :] = table[2 + base + i : 3 + base + i, c * 128 : (c + 1) * 128]


def finish_input_kernel(lens, keep, sent, got, final, d_input, pooled, output):
    half = keep.shape[0]
    output[...] = final[...]
    d_input[...] = keep[...] + got[0:half, :]
    total = sent[half:, :] + got[half:, :]
    for t in range(lens.shape[1]):
        pooled[t : t + 1, :] = total[t : t + 1, :] / lens[0, t].astype(F32)


def swap(x, axis="seq"):
    return lax.ppermute(x, axis, [(0, 1), (1, 0)])


def send_to(x, phase, order, count):
    pairs = []
    for d in range(count):
        for s in range(2):
            pairs.append((2 * d + s, 2 * (d ^ (1 << order[s][phase])) + s))
    return lax.ppermute(x, ("dp", "seq"), pairs)


class Part:
    def __init__(self, keep, send, order, vec):
        self.keep, self.sent, self.order, self.vec, self.got = keep, send, order, vec, None


class Sum:
    def __init__(self, line, parts, count, name):
        self.line, self.parts, self.count, self.name = line, parts, count, name
        self.phase = 0
        self.send()

    def send(self):
        for part in self.parts:
            if self.phase == len(part.order[0]):
                part.got = swap(part.sent)
            else:
                part.got = send_to(part.sent, self.phase, part.order, self.count)

    def step(self):
        last = self.phase == len(self.parts[0].order[0]) - 1
        dtype = F32 if last else BF
        args, outs, scratch, jobs = [], [], [], []
        for part in self.parts:
            rows, cols = part.keep.shape
            half = rows // 2
            extra = 0 if part.vec is None else vector_rows(part.vec.shape[1], cols)
            args += [part.got, part.keep]
            outs += [sds((half, cols), dtype), sds((half + (extra // 2 if last else extra), cols), dtype)]
            if last:
                scratch.append(pltpu.VMEM((rows, cols), F32))
            if part.vec is None:
                jobs.append((last_kernel if last else functools.partial(merge_kernel, rows), 2, 2))
            elif last:
                args.append(part.vec)
                jobs.append((last_vec_kernel, 3, 2))
            else:
                args.append(part.vec)
                outs.append(sds(part.vec.shape, F32))
                jobs.append((functools.partial(merge_vec_kernel, rows), 3, 3))

        def kernel(*refs):
            i, o, t = 0, len(args), len(args) + len(outs)
            for run, reads, writes in jobs:
                run(*refs[i : i + reads], *refs[o : o + writes], *([refs[t]] if last else []))
                i, o, t = i + reads, o + writes, t + 1

        made = self.line.call(
            kernel, outs, *args, scratch=scratch, name=f"sum_{self.name}_{self.phase}", vmem=10, us=MERGE_US
        )
        made = list(made)
        for part, (_, _, writes) in zip(self.parts, jobs):
            part.keep, part.sent = made[0], made[1]
            if writes == 3:
                part.vec = made[2]
            del made[:writes]
        self.phase += 1
        self.send()


def interleave(keep, got, s, pieces):
    size = keep.shape[1] // pieces
    outs = []
    for i in range(pieces):
        a, b = keep[:, i * size : (i + 1) * size], got[:, i * size : (i + 1) * size]
        outs += [jnp.where(s == 0, a, b), jnp.where(s == 0, b, a)]
    return outs


def on_device(
    spread, count,
    hidden_in, w_qkv, b_qv, w_o, b_o, ln1_gain, ln1_bias, w_in, b_in, w_out, b_out, ln2_gain, ln2_bias,
    seg_lengths, cotangent,
):
    row_count, half, width = hidden_in.shape
    length = 2 * half
    mine = width // 2
    heads = HEADS // 2
    ff = w_in.shape[1]
    s = lax.axis_index("seq")
    own = hidden_in.reshape(half, width)
    cot = cotangent.reshape(half, width)
    line = Line()
    call = line.call
    flat = lambda x: x.reshape(1, -1)
    rows_ff, rows_w = ff // GROUPS, width // GROUPS
    half_ff, half_w = GROUPS // 2 * rows_ff, GROUPS // 2 * rows_w
    made, sums, flats = {}, {}, {}

    def parts_of(weight):
        names = [n for n in PARTS if PARTS[n][0] == weight]
        return names, tuple(
            (PARTS[n][1], PARTS[n][2], as_bits(*PARTS[n][3:]) if spread else None) for n in names
        )

    def reduce(names, arrays):
        for i, name in enumerate(names):
            keep, send = arrays[2 * i], arrays[2 * i + 1]
            vec = made["table"] if name == WITH_VECTORS else None
            sums[name] = Part(keep, send, as_bits(*PARTS[name][3:]), vec)
        if spread:
            weight = PARTS[names[0]][0]
            sums[weight] = Sum(line, [sums[n] for n in names], count, weight)

    other = swap(own)
    own, w_mine, bias, lin = call(
        project_kernel,
        [sds((half, width), BF), sds((3, width, mine), BF), sds((8, mine), F32), sds((half, 3 * mine), F32)],
        own, w_qkv, b_qv,
        hbm=(0, 1, 2), scratch=[pltpu.VMEM(b_qv.shape, BF), pltpu.SemaphoreType.DMA((3 * PIECES + 2,))],
        name="project", vmem=12,
    )
    q, k, v, kt, expo, scale, att_t, att_mine, w_o, w_in, w_out = call(
        attend_kernel,
        [sds((length, mine), BF)] * 3
        + [sds((mine, length), BF), sds((heads, length, length), BF), sds((8, length), F32)]
        + [sds((mine, length), F32), sds((length, mine), BF)]
        + [sds(w.shape, BF) for w in (w_o, w_in, w_out)],
        seg_lengths, other, w_mine, bias, lin, w_o, w_in, w_out,
        smem=(0,), hbm=(5, 6, 7), scratch=[pltpu.SemaphoreType.DMA((3 * PIECES,))], name="attend", vmem=16,
    )
    att_got = swap(att_mine)
    (mid_low, active, pull, normal, inverse, sum2, down_own, down_send, output, pool_part, vec_f) = call(
        forward_kernel,
        [
            sds((half, width), BF), sds((half, ff), BF), sds((half, ff), F32), sds((half, width), F32),
            sds((half, 1), F32), sds((half, width), F32), sds((half, mine), BF), sds((half, mine), BF),
            sds((half, width), BF), sds((8, width), F32), sds((8, width), F32),
        ],
        seg_lengths, own, att_mine, att_got, w_o, flat(b_o), flat(ln1_gain), flat(ln1_bias), w_in, flat(b_in),
        w_out, flat(b_out), flat(ln2_gain), flat(ln2_bias), cot,
        smem=(0,), scratch=[pltpu.VMEM((half, width), F32)], name="forward", vmem=16,
    )
    active_got = swap(active)
    mid_got = swap(mid_low)
    down_got = swap(down_send)

    def backward():
        made["up_own"], up_send, made["sum1"], branch, made["vec_b"] = call(
            backward_kernel,
            [
                sds((half, ff // 2), BF), sds((half, ff // 2), BF), sds((half, width), F32),
                sds((half, width), BF), sds((8, width), F32),
            ],
            sum2, pull, normal, inverse, flat(ln1_gain), w_in, w_out,
            scratch=[pltpu.VMEM((half, width), F32)], name="backward", vmem=12,
        )
        made["branch"] = branch, swap(branch)
        made["up_got"] = swap(up_send)

    def grad_out():
        names, parts = parts_of("out")
        outs = [sds((half_ff, stop - start), BF) for start, stop, _ in parts for _ in range(2)]
        arrays = call(
            functools.partial(grad_out_kernel, parts), outs,
            active, active_got, down_own, down_got, name="grad_out",
            scratch=[pltpu.VMEM((ff, mine), BF)],
        )
        reduce(names, arrays)

    def grad_in():
        names, parts = parts_of("in")
        with_o = names.index(WITH_O)
        outs = []
        for i, (start, stop, _) in enumerate(parts):
            outs += [sds((half_w, stop - start + (mine if i == with_o else 0)), BF)] * 2
        arrays = call(
            functools.partial(grad_in_kernel, parts, with_o), outs,
            mid_low, mid_got, made["up_own"], made["up_got"], att_mine, att_got, *made["branch"], name="grad_in",
            scratch=[pltpu.VMEM((width, ff // 2), BF), pltpu.VMEM((width, mine), BF)],
        )
        reduce(names, arrays)

    def attend_back():
        made["grads"], made["vec_a"] = call(
            attend_back_kernel, [sds((length, 3 * mine), BF), sds((8, mine), F32)],
            *made["branch"], w_o, q, k, v, kt, expo, scale, att_t, name="attend_back", vmem=16,
        )

    def grad_qkv():
        names, parts = parts_of("qkv")
        with_vectors = names.index(WITH_VECTORS)
        outs = []
        for i, (start, stop, _) in enumerate(parts):
            extra = vector_rows(width, stop - start) if i == with_vectors else 0
            outs += [sds((half_w, stop - start), BF), sds((half_w + extra, stop - start), BF)]
        outs.append(sds((16, width), F32))
        *arrays, made["table"] = call(
            functools.partial(grad_qkv_kernel, parts, with_vectors), outs,
            own, other, made["grads"], vec_f, made["vec_b"], made["vec_a"], name="grad_qkv",
            scratch=[pltpu.VMEM((width, 3 * mine), BF)],
        )
        reduce(names, arrays)

    def grad_input():
        made["keep"], made["send"] = call(
            grad_input_kernel, [sds((half, width), F32), sds((half + 8, width), F32)],
            made["grads"], w_mine, made["sum1"], pool_part, name="grad_input",
        )
        made["got"] = swap(made["send"])

    def finish_input():
        made["d_input"], made["pooled"], made["output"] = call(
            finish_input_kernel,
            [sds((half, width), F32), sds((seg_lengths.shape[1], width), F32), sds((half, width), BF)],
            seg_lengths, made["keep"], made["send"], made["got"], output, smem=(0,), name="finish_input", end=True,
        )

    def places_of(weight, pieces):
        if weight == "o":
            start, stop = PARTS[WITH_O][1:3]
            return [WITH_O], [(0, stop - start + c) for c in range(0, mine, 128)]
        names, parts = parts_of(weight)
        return names, [
            (i, c - start) for i, (start, stop, _) in enumerate(parts) for c in range(start, stop, 128)
        ]

    def finish_all():
        args, outs, jobs = [], [], []
        for weight, pieces in WEIGHTS.items():
            names, places = places_of(weight, pieces)
            first = len(args)
            args += [x for n in names for x in (sums[n].keep, sums[n].got)]
            outs.append(sds((2 * args[first].shape[0] * len(places), 128), F32))
            jobs.append((functools.partial(finish_kernel, pieces, places), first, len(args)))
        part = sums[WITH_VECTORS]
        one = sds((width // 128, 128), F32)
        args += [part.sent, part.got]
        outs += [sds((2, width), F32), one, one, one, sds((ff // 128, 128), F32), one, one, one]

        def kernel(*refs):
            results = refs[len(args) :]
            sent, got = refs[len(args) - 2 : len(args)]
            for job, (run, start, stop) in enumerate(jobs):
                run(*refs[start:stop], results[job])
            finish_vectors_kernel(part.keep.shape[0], width, sent, got, *results[len(jobs) :])

        done = call(kernel, outs, *args, name="finish", vmem=10)
        for weight, out in zip(WEIGHTS, done):
            flats[weight] = out.reshape(-1)
        made["vectors"] = done[len(jobs) :]

    work = {
        "BWD": backward, "OUT": grad_out, "IN": grad_in, "BACK": attend_back, "QKV": grad_qkv, "INPUT": grad_input,
        "input": finish_input,
    }
    for item in PLAN:
        if item in work:
            work[item]()
        elif spread:
            sums[item].step()
    if spread:
        finish_all()

    if spread:
        vectors = [v if v.shape[0] == 2 else v.reshape(-1) for v in made["vectors"]]
    else:
        for name in PARTS:
            part = sums[name]
            both = jnp.concatenate([part.keep, part.sent[: part.keep.shape[0]]], axis=0)
            total = lax.psum_scatter(both, "dp", scatter_dimension=0, tiled=True).astype(F32)
            half_rows = total.reshape(2, -1, total.shape[1])
            part.keep = jnp.where(s == 0, half_rows[0], half_rows[1])
            part.got = swap(jnp.where(s == 0, half_rows[1], half_rows[0]))
        for weight, pieces in WEIGHTS.items():
            names, places = places_of(weight, pieces)
            keep, got = (
                jnp.concatenate([getattr(sums[names[p]], k)[:, c : c + 128] for p, c in places], axis=1)
                for k in ("keep", "got")
            )
            flats[weight] = jnp.concatenate(interleave(keep, got, s, pieces), axis=1).reshape(-1)
        vec = lax.psum(made["table"], ("dp", "seq"))
        base = ff // width
        vectors = [vec[0:2]] + [vec[2 + base + i] for i in (2, 0, 1)] + [vec[2 : 2 + base].reshape(-1)]
        vectors += [vec[2 + base + i] for i in (5, 3, 4)]
    return (
        made["output"].reshape(row_count, half, width),
        made["pooled"][None],
        made["d_input"].reshape(row_count, half, width),
        *(flats[n] for n in ("qkv", "o", "in", "out")),
        *vectors,
    )


def as_bits(*orders):
    bits = {"x": 0, "y": 1, "1": 2, "2": 3}
    return tuple(tuple(bits[c] for c in order) for order in orders)


def solution(mesh):
    count = mesh.shape["dp"]
    in_specs = (P("dp", "seq", None),) + (P(),) * 12 + (P("dp", None), P("dp", "seq", None))
    out_specs = (
        P("dp", "seq", None),
        P("dp", None, None),
        P("dp", "seq", None),
    ) + (P(("dp", "seq")),) * 4 + (P(),) * 8
    return jax.shard_map(
        functools.partial(on_device, count == GROUPS, count),
        mesh=mesh, in_specs=in_specs, out_specs=out_specs, check_vma=False,
    )
```

```python
import functools
import math

import jax
import jax.numpy as jnp
from jax import lax
from jax.experimental import pallas as pl
from jax.experimental.pallas import tpu as pltpu
from jax.sharding import PartitionSpec as P

HEADS = 12
EPSILON = 1e-12
HIDE = -1e30
GROUPS = 16
BF = jnp.bfloat16
F32 = jnp.float32
MIB = 2**20
PIECES = 1
MERGE_US = 1.0
KERNEL_US = 1.0
WEIGHTS = {"out": 1, "in": 1, "qkv": 3, "o": 1}
PARTS = {
    "a": ("out", 0, 384, "y1x2", "12yx"),
    "b": ("in", 0, 1024, "y1x2", "xy12"),
    "c": ("in", 1024, 1536, "1yx2", "yx21"),
    "d": ("qkv", 0, 1152, "x2y1", "xy12"),
}
WITH_O = "c"
WITH_VECTORS = "d"
PLAN = (
    "BWD", "OUT", "BACK", "QKV", "IN", "INPUT", "out", "qkv", "in", "input", "out", "qkv",
    "in", "out", "qkv", "in", "out", "qkv", "in",
)


def sds(shape, dtype):
    return jax.ShapeDtypeStruct(shape, dtype)


def nn(left, right):
    return jnp.dot(left, right, preferred_element_type=F32)


def nt(left, right):
    return lax.dot_general(left, right, (((1,), (1,)), ((), ())), preferred_element_type=F32)


def tn(left, right):
    return lax.dot_general(left, right, (((0,), (0,)), ((), ())), preferred_element_type=F32)


class Line:
    def __init__(self):
        self.last = None

    def call(self, kernel, outs, *args, scratch=(), hbm=(), smem=(), name=None, vmem=16, us=KERNEL_US, end=False):
        if end:
            outs = [sds((8, 128), F32), *outs]
        specs = []
        lead = len(args)
        for i in range(lead):
            space = pltpu.HBM if i in hbm else pltpu.SMEM if i in smem else pltpu.VMEM
            specs.append(pl.BlockSpec(memory_space=space))
        args = [
            pltpu.with_memory_space_constraint(arg, pltpu.HBM) if i in hbm else arg
            for i, arg in enumerate(args)
        ]
        after = () if self.last is None else (self.last,)
        specs += [pl.BlockSpec(memory_space=pl.ANY) for _ in after]

        def body(*refs):
            rest = refs[lead + len(after) :]
            if end:
                rest[0][...] = jnp.zeros((8, 128), F32)
                rest = rest[1:]
            kernel(*refs[:lead], *rest)

        made = pl.pallas_call(
            body,
            out_shape=list(outs),
            in_specs=specs,
            out_specs=[pl.BlockSpec(memory_space=pltpu.VMEM) for _ in outs],
            scratch_shapes=list(scratch),
            compiler_params=pltpu.CompilerParams(vmem_limit_bytes=vmem * MIB),
            cost_estimate=pl.CostEstimate(flops=int(us * 1.1e9), bytes_accessed=1024, transcendentals=0),
            name=name,
        )(*args, *after)
        self.last = made[0]
        return made[1:] if end else made


def segment_of(positions, lens_ref):
    ids = jnp.zeros_like(positions)
    end = jnp.int32(0)
    for j in range(lens_ref.shape[1]):
        end = end + lens_ref[0, j]
        ids = ids + (positions >= end).astype(jnp.int32)
    return ids


def own_first(index, half, s):
    return jnp.where(index < half, index + s * half, index - half + (1 - s) * half)


def normalise(total):
    centered = total - jnp.mean(total, axis=-1, keepdims=True)
    inverse = lax.rsqrt(jnp.mean(centered * centered, axis=-1, keepdims=True) + EPSILON)
    return centered * inverse, inverse


def norm_pull(grad, normal, inverse, gain):
    scaled = grad * gain
    return inverse * (
        scaled
        - jnp.mean(scaled, axis=-1, keepdims=True)
        - normal * jnp.mean(scaled * normal, axis=-1, keepdims=True)
    )


def column_sum(matrix):
    return jnp.sum(matrix, axis=0, keepdims=True)


def copies_of(source, target, sems, first, pieces):
    rows = target.shape[0] // pieces
    return [
        pltpu.make_async_copy(
            source.at[i * rows : (i + 1) * rows, :], target.at[i * rows : (i + 1) * rows, :], sems.at[first + i]
        )
        for i in range(pieces)
    ]


def project_kernel(own_hbm, w_hbm, b_hbm, own, w_mine, bias, lin, b_buf, sems):
    width = own.shape[1]
    mine = width // 2
    s = lax.axis_index("seq")
    first = pltpu.make_async_copy(own_hbm, own, sems.at[3 * PIECES])
    first.start()
    copies = []
    for c in range(3):
        start = pl.multiple_of(c * width + s * mine, 128)
        copies.append(copies_of(w_hbm.at[:, pl.ds(start, mine)], w_mine.at[c], sems, c * PIECES, PIECES))
        for copy in copies[-1]:
            copy.start()
    second = pltpu.make_async_copy(b_hbm, b_buf, sems.at[3 * PIECES + 1])
    second.start()
    second.wait()
    column = pl.ds(pl.multiple_of(s * mine, 128), mine)
    bias[...] = jnp.zeros_like(bias)
    bias[0:1, :] = b_buf[0:1, column].astype(F32)
    bias[2:3, :] = b_buf[1:2, column].astype(F32)
    first.wait()
    for c in range(3):
        for copy in copies[c]:
            copy.wait()
        lin[:, c * mine : (c + 1) * mine] = nn(own[...], w_mine[c]) + bias[c : c + 1, :]


def attend_kernel(
    lens, other, w_mine, bias, lin, w_o_hbm, w_in_hbm, w_out_hbm,
    q_out, k_out, v_out, kt_out, expo_out, scale_out, att_t, att_out, w_o, w_in, w_out, sems,
):
    half, width = other.shape
    length = 2 * half
    mine = width // 2
    pair = 2 * (width // HEADS)
    head = pair // 2
    s = lax.axis_index("seq")
    copies = []
    for source, target in ((w_o_hbm, w_o), (w_in_hbm, w_in), (w_out_hbm, w_out)):
        copies += copies_of(source, target, sems, len(copies), PIECES)
    for copy in copies:
        copy.start()
    parts = []
    for c in range(3):
        rest = nn(other[...], w_mine[c]) + bias[c : c + 1, :]
        parts.append(jnp.concatenate([lin[:, c * mine : (c + 1) * mine], rest], axis=0))
    q_all, k_all, v_all = parts
    q_all = q_all.astype(BF).astype(F32) * (1.0 / math.sqrt(head))
    q_out[...] = q_all.astype(BF)
    k_out[...] = k_all.astype(BF)
    v_out[...] = v_all.astype(BF)
    kt_out[...] = k_all.T.astype(BF)
    vt = v_all.T.astype(BF)
    rows = own_first(lax.broadcasted_iota(jnp.int32, (length, pair), 0), half, s)
    lane = lax.broadcasted_iota(jnp.int32, (length, pair), 1)
    same = segment_of(rows, lens) == lane % head
    in_range = lane % head < lens.shape[1]
    mark_k = jnp.where(same, 1.0, 0.0)
    mark_q = jnp.where(jnp.logical_and(in_range, jnp.logical_not(same)), HIDE, 0.0)
    first = lane < head
    for j in range(mine // pair):
        cols = slice(j * pair, (j + 1) * pair)
        q2, k2 = q_all[:, cols], k_all[:, cols]
        pieces = []
        for a in range(2):
            keep = first if a == 0 else jnp.logical_not(first)
            k_m = jnp.where(keep, k2, mark_k).astype(BF)
            q_m = jnp.where(keep, q2, mark_q).astype(BF)
            scores = nt(k_m, q_m)
            top = jnp.max(scores, axis=0, keepdims=True)
            expo = jnp.exp(scores - top)
            scale = 1.0 / jnp.sum(expo, axis=0, keepdims=True)
            low = expo.astype(BF)
            h = 2 * j + a
            expo_out[h] = low
            scale_out[h : h + 1, :] = scale
            pieces.append(nn(vt[h * head : (h + 1) * head, :], low) * scale)
        both = jnp.concatenate(pieces, axis=0)
        att_t[cols, :] = both
        att_out[:, cols] = both.T.astype(BF)
    for copy in copies:
        copy.wait()


def forward_kernel(
    lens,
    own,
    att_mine,
    att_got,
    w_o,
    b_o,
    gain1,
    shift1,
    w_in,
    b_in,
    w_out,
    b_out,
    gain2,
    shift2,
    cot,
    mid_out,
    active_out,
    pull_out,
    normal_out,
    inverse_out,
    sum2_out,
    down_keep,
    down_send,
    out_out,
    pool_out,
    vec_out,
    down_acc,
):
    half, width = own.shape
    mine = width // 2
    ff = w_in.shape[1]
    s = lax.axis_index("seq")
    row_a = pl.ds(pl.multiple_of(s * mine, 128), mine)
    row_b = pl.ds(pl.multiple_of((1 - s) * mine, 128), mine)
    branch = nn(att_mine[0:half, :], w_o[row_a, :]) + nn(att_got[half:, :], w_o[row_b, :])
    normal, inverse = normalise(own[...].astype(F32) + (branch + b_o[...].astype(F32)))
    middle = normal * gain1[...].astype(F32) + shift1[...].astype(F32)
    low = middle.astype(BF)
    mid_out[...] = low
    normal_out[...] = normal
    inverse_out[...] = inverse
    down_acc[...] = middle + b_out[...].astype(F32)
    step = 1024
    for c in range(0, ff, step):
        cols = slice(c, c + step)
        upper = nn(low, w_in[:, cols]) + b_in[:, cols].astype(F32)
        cdf = 0.5 + 0.5 * lax.erf(upper * (1.0 / math.sqrt(2.0)))
        density = jnp.exp(-0.5 * upper * upper) * (1.0 / math.sqrt(2.0 * math.pi))
        act = (upper * cdf).astype(BF)
        active_out[:, cols] = act
        pull_out[:, cols] = cdf + upper * density
        down_acc[...] += nn(act, w_out[cols, :])
    normal2, inverse2 = normalise(down_acc[...])
    gain = gain2[...].astype(F32)
    final = normal2 * gain + shift2[...].astype(F32)
    out_out[...] = final.astype(BF)
    rows = lax.broadcasted_iota(jnp.int32, (half, 1), 0) + s * half
    ids = segment_of(rows, lens)
    pool_out[...] = jnp.zeros_like(pool_out)
    for t in range(lens.shape[1]):
        pool_out[t : t + 1, :] = column_sum(jnp.where(ids == t, final, 0.0))
    grad = cot[...].astype(F32)
    sum2 = norm_pull(grad, normal2, inverse2, gain)
    sum2_out[...] = sum2
    down = sum2.astype(BF)
    down_acc[...] = sum2
    down_keep[...] = down_acc[:, row_a].astype(BF)
    down_send[...] = down_acc[:, row_b].astype(BF)
    vec_out[...] = jnp.zeros_like(vec_out)
    vec_out[0:1, :] = column_sum(grad * normal2)
    vec_out[1:2, :] = column_sum(grad)
    vec_out[2:3, :] = column_sum(down.astype(F32))


def backward_kernel(
    sum2, pull, normal, inverse, gain1, w_in, w_out,
    up_keep, up_send, sum1_out, branch_out, vec_out, mid_acc,
):
    width, ff = w_in.shape
    s = lax.axis_index("seq")
    step = 768
    per = ff // 2 // step
    mid_acc[...] = sum2[...]
    low = sum2[...].astype(BF)
    vec_out[...] = jnp.zeros_like(vec_out)
    sums = []
    for i in range(2 * per):
        block = (i // per + s) % 2
        start = pl.multiple_of(block * (ff // 2) + (i % per) * step, 128)
        cols = pl.ds(start, step)
        grad_upper = (nt(low, w_out[cols, :]) * pull[:, cols]).astype(BF)
        place = up_keep if i < per else up_send
        place[:, (i % per) * step : (i % per + 1) * step] = grad_upper
        sums.append(column_sum(grad_upper.astype(F32)))
        mid_acc[...] += nt(grad_upper, w_in[:, cols])
    ups = [jnp.concatenate(sums[:per], axis=1), jnp.concatenate(sums[per:], axis=1)]
    for b in range(2):
        line = jnp.where(s == b, ups[0], ups[1])
        for r in range(ff // 2 // width):
            row = b * (ff // 2 // width) + r
            vec_out[row : row + 1, :] = line[:, r * width : (r + 1) * width]
    base = ff // width
    grad_mid = mid_acc[...]
    vec_out[base : base + 1, :] = column_sum(grad_mid * normal[...])
    vec_out[base + 1 : base + 2, :] = column_sum(grad_mid)
    sum1 = norm_pull(grad_mid, normal[...], inverse[...], gain1[...].astype(F32))
    sum1_out[...] = sum1
    branch = sum1.astype(BF)
    branch_out[...] = branch
    vec_out[base + 2 : base + 3, :] = column_sum(branch.astype(F32))


def attend_back_kernel(
    branch_own, branch_got, w_o, q, k, v, kt, expo, scale, att_t, grad_out, vec_out
):
    length, mine = q.shape
    width = w_o.shape[1]
    head = width // HEADS
    pair = 2 * head
    s = lax.axis_index("seq")
    w_mine = w_o[pl.ds(pl.multiple_of(s * mine, 128), mine), :]
    grad_t = jnp.concatenate([nt(w_mine, branch_own[...]), nt(w_mine, branch_got[...])], axis=1)
    lane = lax.broadcasted_iota(jnp.int32, (length, pair), 1)
    first = lane < head
    vec_out[...] = jnp.zeros_like(vec_out)
    for j in range(mine // pair):
        cols = slice(j * pair, (j + 1) * pair)
        q2 = q[:, cols]
        v2 = v[:, cols].astype(F32)
        scaled, inners = [], []
        for h in (2 * j, 2 * j + 1):
            part = slice(h * head, (h + 1) * head)
            times = scale[h : h + 1, :]
            scaled.append(grad_t[part, :] * times)
            inners.append(jnp.sum(att_t[part, :] * scaled[-1], axis=0, keepdims=True))
        a2 = jnp.concatenate(scaled, axis=0).astype(BF)
        dq, dk, dv = [], [], []
        for a in range(2):
            h = 2 * j + a
            keep = first if a == 0 else jnp.logical_not(first)
            v_m = jnp.where(keep, v2, 0.0).astype(BF)
            grad_p = nn(v_m, a2)
            low = expo[h]
            raw = (low.astype(F32) * (grad_p - inners[a])).astype(BF)
            dk.append(nn(raw, q2))
            dv.append(nt(low, a2))
            dq.append(nn(kt[h * head : (h + 1) * head, :], raw))
        dq_low = (jnp.concatenate(dq, axis=0) * (1.0 / math.sqrt(head))).astype(BF).T
        dk_low = jnp.where(first, dk[0], dk[1]).astype(BF)
        dv_low = jnp.where(first, dv[0], dv[1]).astype(BF)
        grad_out[:, cols] = dq_low
        grad_out[:, mine + j * pair : mine + (j + 1) * pair] = dk_low
        grad_out[:, 2 * mine + j * pair : 2 * mine + (j + 1) * pair] = dv_low
        vec_out[0:1, cols] = column_sum(dq_low.astype(F32))
        vec_out[1:2, cols] = column_sum(dv_low.astype(F32))


def chunk_of(slot, order):
    if order is None:
        return slot
    chunks = []
    for bits in order:
        rel = 0
        for i, bit in enumerate(bits):
            rel |= (slot >> (len(bits) - 1 - i) & 1) << bit
        chunks.append(rel)
    rel = jnp.where(lax.axis_index("seq") == 0, jnp.int32(chunks[0]), jnp.int32(chunks[1]))
    return jnp.bitwise_xor(rel, lax.axis_index("dp"))


def spread_rows(whole, order, keep, send, cols, to):
    rows = whole.shape[0] // GROUPS
    for slot in range(GROUPS):
        chunk = chunk_of(slot, order)
        target = keep if slot < GROUPS // 2 else send
        place = slot % (GROUPS // 2) * rows
        target[place : place + rows, to] = whole[pl.ds(pl.multiple_of(chunk * rows, 16), rows), cols]


def grad_out_kernel(parts, active_own, active_got, down_own, down_got, *outs):
    *outs, whole = outs
    block = 512
    for i in range(0, active_own.shape[1], block):
        cols = slice(i, i + block)
        whole[cols, :] = (
            tn(active_own[:, cols], down_own[...]) + tn(active_got[:, cols], down_got[...])
        ).astype(BF)
    for p, (start, stop, order) in enumerate(parts):
        spread_rows(whole, order, outs[2 * p], outs[2 * p + 1], slice(start, stop), slice(0, stop - start))


def grad_in_kernel(
    parts, with_o, mid_own, mid_got, up_own, up_got, att_mine, att_got, branch_own, branch_got, *outs
):
    *outs, whole, whole_o = outs
    half, width = mid_own.shape
    mine = width // 2
    for i in range(2):
        cols = slice(i * mine, (i + 1) * mine)
        own_t, got_t = mid_own[:, cols].T, mid_got[:, cols].T
        for n in range(0, up_own.shape[1], 512):
            out = slice(n, n + 512)
            whole[cols, out] = (nn(own_t, up_own[:, out]) + nn(got_t, up_got[:, out])).astype(BF)
    s = lax.axis_index("seq")
    column = pl.ds(pl.multiple_of(s * mine, 128), mine)
    mine_o = tn(att_mine[0:half, :], branch_own[:, column]) + tn(att_mine[half:, :], branch_got[:, column])
    got_o = tn(att_got[half:, :], branch_own[:, column]) + tn(att_got[0:half, :], branch_got[:, column])
    for i in range(2):
        whole_o[i * mine : (i + 1) * mine, :] = jnp.where(s == i, mine_o, got_o).astype(BF)
    for p, (start, stop, order) in enumerate(parts):
        spread_rows(whole, order, outs[2 * p], outs[2 * p + 1], slice(start, stop), slice(0, stop - start))
        if p == with_o:
            to = slice(stop - start, stop - start + mine)
            spread_rows(whole_o, order, outs[2 * p], outs[2 * p + 1], slice(0, mine), to)


USED = 12


def pack_vectors(table, send, start):
    total = table.shape[1]
    high = table.astype(BF).astype(F32)
    rest = (table - high).astype(BF).astype(F32)
    half = total // 2
    if send.shape[1] >= total + half:
        more = jnp.concatenate([rest[4:8, half:], rest[8:USED, half:]], axis=1)
        send[start : start + 16, 0:total] = jnp.concatenate([high[0:USED, :], more], axis=0).astype(BF)
        side = jnp.concatenate([rest[0:USED, 0:half], rest[0:4, half:]], axis=0)
        send[start : start + 16, total : total + half] = side.astype(BF)
    else:
        width = min(total, send.shape[1])
        row = start
        for piece in (high, rest):
            for c in range(0, total, width):
                send[row : row + 16, 0:width] = piece[:, c : c + width].astype(BF)
                row += 16
    return high + rest


def unpack_vectors(got, start, total):
    half = total // 2
    if got.shape[1] >= total + half:
        first = got[start : start + 16, 0:total].astype(F32)
        side = got[start : start + 16, total : total + half].astype(F32)
        right = jnp.concatenate([side[USED:, :], first[USED:, 0:half], first[USED:, half:]], axis=0)
        rest = jnp.concatenate([side[0:USED, :], right], axis=1)
        return jnp.concatenate([first[0:USED, :] + rest, jnp.zeros((16 - USED, total), F32)], axis=0)
    width = min(total, got.shape[1])
    count = total // width
    parts = [got[start + 16 * i : start + 16 * (i + 1), 0:width].astype(F32) for i in range(2 * count)]
    return jnp.concatenate([parts[i] + parts[count + i] for i in range(count)], axis=1)


def vector_rows(total, cols, whole=False):
    pieces = total // min(total, cols)
    return 16 * pieces * (1 if whole or cols >= total + total // 2 else 2)


def grad_qkv_kernel(parts, with_vectors, own, other, grads, vec_f, vec_b, vec_a, *outs):
    *outs, whole = outs
    half, width = own.shape
    mine = width // 2
    rows = width // GROUPS
    s = lax.axis_index("seq")
    for i in range(2):
        cols = slice(i * mine, (i + 1) * mine)
        both_t = jnp.concatenate([own[:, cols].T, other[:, cols].T], axis=1)
        for c in range(3):
            out = slice(c * mine, (c + 1) * mine)
            whole[cols, out] = nn(both_t, grads[:, out]).astype(BF)
    for p, (start, stop, order) in enumerate(parts):
        spread_rows(whole, order, outs[2 * p], outs[2 * p + 1], slice(start, stop), slice(0, stop - start))
    zero = jnp.zeros((1, mine), F32)
    lines = []
    for r in range(2):
        line = vec_a[r : r + 1, :]
        lines.append(
            jnp.concatenate([jnp.where(s == 0, line, zero), jnp.where(s == 0, zero, line)], axis=1)
        )
    table = jnp.concatenate(lines + [vec_b[0:7, :], vec_f[0:3, :], jnp.zeros((4, width), F32)], axis=0)
    outs[-1][...] = pack_vectors(table, outs[2 * with_vectors + 1], GROUPS // 2 * rows)


def grad_input_kernel(grads, w_mine, sum1, pool, keep, send):
    half, width = sum1.shape
    mine = width // 2
    a, b = sum1[...], jnp.zeros((half, width), F32)
    for c in range(3):
        cols = slice(c * mine, (c + 1) * mine)
        a = a + nt(grads[0:half, cols], w_mine[c])
        b = b + nt(grads[half:, cols], w_mine[c])
    keep[...] = a
    send[0:half, :] = b
    send[half:, :] = pool[...]


def merge_kernel(rows, got, keep, keep_out, send_out):
    total = keep[0:rows, :].astype(F32) + got[0:rows, :].astype(F32)
    keep_out[...] = total[0 : rows // 2, :].astype(BF)
    send_out[...] = total[rows // 2 :, :].astype(BF)


def merge_vec_kernel(rows, got, keep, vec, keep_out, send_out, vec_out):
    merge_kernel(rows, got, keep, keep_out, send_out.at[0 : rows // 2, :])
    table = vec[...] + unpack_vectors(got, rows, vec.shape[1])
    vec_out[...] = pack_vectors(table, send_out, rows // 2)


def last_kernel(got, keep, keep_out, send_out, acc):
    rows = keep.shape[0]
    s = lax.axis_index("seq")
    acc[...] = keep[...].astype(F32) + got[0:rows, :].astype(F32)
    keep_out[...] = acc[pl.ds(pl.multiple_of(s * (rows // 2), 8), rows // 2), :]
    send_out[...] = acc[pl.ds(pl.multiple_of((1 - s) * (rows // 2), 8), rows // 2), :]


def last_vec_kernel(got, keep, vec, keep_out, send_out, acc):
    rows = keep.shape[0]
    last_kernel(got, keep, keep_out, send_out.at[0 : rows // 2, :], acc)
    table = vec[...] + unpack_vectors(got, rows, vec.shape[1])
    width = min(table.shape[1], keep.shape[1])
    for i, c in enumerate(range(0, table.shape[1], width)):
        send_out[rows // 2 + 16 * i : rows // 2 + 16 * (i + 1), 0:width] = table[:, c : c + width]


def finish_kernel(pieces, places, *refs):
    flat = refs[-1]
    count = len(places)
    per = count // pieces
    s = lax.axis_index("seq")
    for j, (p, lane) in enumerate(places):
        keep, got = refs[2 * p], refs[2 * p + 1]
        rows = keep.shape[0]
        cols = slice(lane, lane + 128)
        first, second = keep[:, cols], got[0:rows, cols]
        line = j // per * 2 * per + j % per
        flat[pl.ds(line, rows, stride=2 * count), :] = jnp.where(s == 0, first, second)
        flat[pl.ds(line + per, rows, stride=2 * count), :] = jnp.where(s == 0, second, first)


def finish_vectors_kernel(rows, width, sent, got, b_qv, b_o, gain1, shift1, b_in, b_out, gain2, shift2):
    half = min(width, sent.shape[1])
    count = width // half
    total = sent[rows:, 0:half] + got[rows:, 0:half]
    table = jnp.concatenate([total[16 * i : 16 * (i + 1), :] for i in range(count)], axis=1)
    b_qv[...] = table[0:2, :]
    base = b_in.shape[0] * 128 // width
    for r in range(base):
        for c in range(width // 128):
            line = r * (width // 128) + c
            b_in[line : line + 1, :] = table[2 + r : 3 + r, c * 128 : (c + 1) * 128]
    for i, ref in enumerate((gain1, shift1, b_o, gain2, shift2, b_out)):
        for c in range(width // 128):
            ref[c : c + 1, :] = table[2 + base + i : 3 + base + i, c * 128 : (c + 1) * 128]


def finish_input_kernel(lens, keep, sent, got, final, d_input, pooled, output):
    half = keep.shape[0]
    output[...] = final[...]
    d_input[...] = keep[...] + got[0:half, :]
    total = sent[half:, :] + got[half:, :]
    for t in range(lens.shape[1]):
        pooled[t : t + 1, :] = total[t : t + 1, :] / lens[0, t].astype(F32)


def swap(x, axis="seq"):
    return lax.ppermute(x, axis, [(0, 1), (1, 0)])


def send_to(x, phase, order, count):
    pairs = []
    for d in range(count):
        for s in range(2):
            pairs.append((2 * d + s, 2 * (d ^ (1 << order[s][phase])) + s))
    return lax.ppermute(x, ("dp", "seq"), pairs)


class Part:
    def __init__(self, keep, send, order, vec):
        self.keep, self.sent, self.order, self.vec, self.got = keep, send, order, vec, None


class Sum:
    def __init__(self, line, parts, count, name):
        self.line, self.parts, self.count, self.name = line, parts, count, name
        self.phase = 0
        self.send()

    def send(self):
        for part in self.parts:
            if self.phase == len(part.order[0]):
                part.got = swap(part.sent)
            else:
                part.got = send_to(part.sent, self.phase, part.order, self.count)

    def step(self):
        last = self.phase == len(self.parts[0].order[0]) - 1
        dtype = F32 if last else BF
        args, outs, scratch, jobs = [], [], [], []
        for part in self.parts:
            rows, cols = part.keep.shape
            half = rows // 2
            extra = 0 if part.vec is None else vector_rows(part.vec.shape[1], cols, last)
            args += [part.got, part.keep]
            outs += [sds((half, cols), dtype), sds((half + extra, cols), dtype)]
            if last:
                scratch.append(pltpu.VMEM((rows, cols), F32))
            if part.vec is None:
                jobs.append((last_kernel if last else functools.partial(merge_kernel, rows), 2, 2))
            elif last:
                args.append(part.vec)
                jobs.append((last_vec_kernel, 3, 2))
            else:
                args.append(part.vec)
                outs.append(sds(part.vec.shape, F32))
                jobs.append((functools.partial(merge_vec_kernel, rows), 3, 3))

        def kernel(*refs):
            i, o, t = 0, len(args), len(args) + len(outs)
            for run, reads, writes in jobs:
                run(*refs[i : i + reads], *refs[o : o + writes], *([refs[t]] if last else []))
                i, o, t = i + reads, o + writes, t + 1

        made = self.line.call(
            kernel, outs, *args, scratch=scratch, name=f"sum_{self.name}_{self.phase}", vmem=10, us=MERGE_US
        )
        made = list(made)
        for part, (_, _, writes) in zip(self.parts, jobs):
            part.keep, part.sent = made[0], made[1]
            if writes == 3:
                part.vec = made[2]
            del made[:writes]
        self.phase += 1
        self.send()


def interleave(keep, got, s, pieces):
    size = keep.shape[1] // pieces
    outs = []
    for i in range(pieces):
        a, b = keep[:, i * size : (i + 1) * size], got[:, i * size : (i + 1) * size]
        outs += [jnp.where(s == 0, a, b), jnp.where(s == 0, b, a)]
    return outs


def on_device(
    spread, count,
    hidden_in, w_qkv, b_qv, w_o, b_o, ln1_gain, ln1_bias, w_in, b_in, w_out, b_out, ln2_gain, ln2_bias,
    seg_lengths, cotangent,
):
    row_count, half, width = hidden_in.shape
    length = 2 * half
    mine = width // 2
    heads = HEADS // 2
    ff = w_in.shape[1]
    s = lax.axis_index("seq")
    own = hidden_in.reshape(half, width)
    cot = cotangent.reshape(half, width)
    line = Line()
    call = line.call
    flat = lambda x: x.reshape(1, -1)
    rows_ff, rows_w = ff // GROUPS, width // GROUPS
    half_ff, half_w = GROUPS // 2 * rows_ff, GROUPS // 2 * rows_w
    made, sums, flats = {}, {}, {}

    def parts_of(weight):
        names = [n for n in PARTS if PARTS[n][0] == weight]
        return names, tuple(
            (PARTS[n][1], PARTS[n][2], as_bits(*PARTS[n][3:]) if spread else None) for n in names
        )

    def reduce(names, arrays):
        for i, name in enumerate(names):
            keep, send = arrays[2 * i], arrays[2 * i + 1]
            vec = made["table"] if name == WITH_VECTORS else None
            sums[name] = Part(keep, send, as_bits(*PARTS[name][3:]), vec)
        if spread:
            weight = PARTS[names[0]][0]
            sums[weight] = Sum(line, [sums[n] for n in names], count, weight)

    other = swap(own)
    own, w_mine, bias, lin = call(
        project_kernel,
        [sds((half, width), BF), sds((3, width, mine), BF), sds((8, mine), F32), sds((half, 3 * mine), F32)],
        own, w_qkv, b_qv,
        hbm=(0, 1, 2), scratch=[pltpu.VMEM(b_qv.shape, BF), pltpu.SemaphoreType.DMA((3 * PIECES + 2,))],
        name="project", vmem=12,
    )
    q, k, v, kt, expo, scale, att_t, att_mine, w_o, w_in, w_out = call(
        attend_kernel,
        [sds((length, mine), BF)] * 3
        + [sds((mine, length), BF), sds((heads, length, length), BF), sds((8, length), F32)]
        + [sds((mine, length), F32), sds((length, mine), BF)]
        + [sds(w.shape, BF) for w in (w_o, w_in, w_out)],
        seg_lengths, other, w_mine, bias, lin, w_o, w_in, w_out,
        smem=(0,), hbm=(5, 6, 7), scratch=[pltpu.SemaphoreType.DMA((3 * PIECES,))], name="attend", vmem=16,
    )
    att_got = swap(att_mine)
    (mid_low, active, pull, normal, inverse, sum2, down_own, down_send, output, pool_part, vec_f) = call(
        forward_kernel,
        [
            sds((half, width), BF), sds((half, ff), BF), sds((half, ff), F32), sds((half, width), F32),
            sds((half, 1), F32), sds((half, width), F32), sds((half, mine), BF), sds((half, mine), BF),
            sds((half, width), BF), sds((8, width), F32), sds((8, width), F32),
        ],
        seg_lengths, own, att_mine, att_got, w_o, flat(b_o), flat(ln1_gain), flat(ln1_bias), w_in, flat(b_in),
        w_out, flat(b_out), flat(ln2_gain), flat(ln2_bias), cot,
        smem=(0,), scratch=[pltpu.VMEM((half, width), F32)], name="forward", vmem=16,
    )
    active_got = swap(active)
    mid_got = swap(mid_low)
    down_got = swap(down_send)

    def backward():
        made["up_own"], up_send, made["sum1"], branch, made["vec_b"] = call(
            backward_kernel,
            [
                sds((half, ff // 2), BF), sds((half, ff // 2), BF), sds((half, width), F32),
                sds((half, width), BF), sds((8, width), F32),
            ],
            sum2, pull, normal, inverse, flat(ln1_gain), w_in, w_out,
            scratch=[pltpu.VMEM((half, width), F32)], name="backward", vmem=12,
        )
        made["branch"] = branch, swap(branch)
        made["up_got"] = swap(up_send)

    def grad_out():
        names, parts = parts_of("out")
        outs = [sds((half_ff, stop - start), BF) for start, stop, _ in parts for _ in range(2)]
        arrays = call(
            functools.partial(grad_out_kernel, parts), outs,
            active, active_got, down_own, down_got, name="grad_out",
            scratch=[pltpu.VMEM((ff, mine), BF)],
        )
        reduce(names, arrays)

    def grad_in():
        names, parts = parts_of("in")
        with_o = names.index(WITH_O)
        outs = []
        for i, (start, stop, _) in enumerate(parts):
            outs += [sds((half_w, stop - start + (mine if i == with_o else 0)), BF)] * 2
        arrays = call(
            functools.partial(grad_in_kernel, parts, with_o), outs,
            mid_low, mid_got, made["up_own"], made["up_got"], att_mine, att_got, *made["branch"], name="grad_in",
            scratch=[pltpu.VMEM((width, ff // 2), BF), pltpu.VMEM((width, mine), BF)],
        )
        reduce(names, arrays)

    def attend_back():
        made["grads"], made["vec_a"] = call(
            attend_back_kernel, [sds((length, 3 * mine), BF), sds((8, mine), F32)],
            *made["branch"], w_o, q, k, v, kt, expo, scale, att_t, name="attend_back", vmem=16,
        )

    def grad_qkv():
        names, parts = parts_of("qkv")
        with_vectors = names.index(WITH_VECTORS)
        outs = []
        for i, (start, stop, _) in enumerate(parts):
            extra = vector_rows(width, stop - start) if i == with_vectors else 0
            outs += [sds((half_w, stop - start), BF), sds((half_w + extra, stop - start), BF)]
        outs.append(sds((16, width), F32))
        *arrays, made["table"] = call(
            functools.partial(grad_qkv_kernel, parts, with_vectors), outs,
            own, other, made["grads"], vec_f, made["vec_b"], made["vec_a"], name="grad_qkv",
            scratch=[pltpu.VMEM((width, 3 * mine), BF)],
        )
        reduce(names, arrays)

    def grad_input():
        made["keep"], made["send"] = call(
            grad_input_kernel, [sds((half, width), F32), sds((half + 8, width), F32)],
            made["grads"], w_mine, made["sum1"], pool_part, name="grad_input",
        )
        made["got"] = swap(made["send"])

    def finish_input():
        made["d_input"], made["pooled"], made["output"] = call(
            finish_input_kernel,
            [sds((half, width), F32), sds((seg_lengths.shape[1], width), F32), sds((half, width), BF)],
            seg_lengths, made["keep"], made["send"], made["got"], output, smem=(0,), name="finish_input", end=True,
        )

    def places_of(weight, pieces):
        if weight == "o":
            start, stop = PARTS[WITH_O][1:3]
            return [WITH_O], [(0, stop - start + c) for c in range(0, mine, 128)]
        names, parts = parts_of(weight)
        return names, [
            (i, c - start) for i, (start, stop, _) in enumerate(parts) for c in range(start, stop, 128)
        ]

    def finish_all():
        args, outs, jobs = [], [], []
        for weight, pieces in WEIGHTS.items():
            names, places = places_of(weight, pieces)
            first = len(args)
            args += [x for n in names for x in (sums[n].keep, sums[n].got)]
            outs.append(sds((2 * args[first].shape[0] * len(places), 128), F32))
            jobs.append((functools.partial(finish_kernel, pieces, places), first, len(args)))
        part = sums[WITH_VECTORS]
        one = sds((width // 128, 128), F32)
        args += [part.sent, part.got]
        outs += [sds((2, width), F32), one, one, one, sds((ff // 128, 128), F32), one, one, one]

        def kernel(*refs):
            results = refs[len(args) :]
            sent, got = refs[len(args) - 2 : len(args)]
            for job, (run, start, stop) in enumerate(jobs):
                run(*refs[start:stop], results[job])
            finish_vectors_kernel(part.keep.shape[0], width, sent, got, *results[len(jobs) :])

        done = call(kernel, outs, *args, name="finish", vmem=10)
        for weight, out in zip(WEIGHTS, done):
            flats[weight] = out.reshape(-1)
        made["vectors"] = done[len(jobs) :]

    work = {
        "BWD": backward, "OUT": grad_out, "IN": grad_in, "BACK": attend_back, "QKV": grad_qkv, "INPUT": grad_input,
        "input": finish_input,
    }
    for item in PLAN:
        if item in work:
            work[item]()
        elif spread:
            sums[item].step()
    if spread:
        finish_all()

    if spread:
        vectors = [v if v.shape[0] == 2 else v.reshape(-1) for v in made["vectors"]]
    else:
        for name in PARTS:
            part = sums[name]
            both = jnp.concatenate([part.keep, part.sent[: part.keep.shape[0]]], axis=0)
            total = lax.psum_scatter(both, "dp", scatter_dimension=0, tiled=True).astype(F32)
            half_rows = total.reshape(2, -1, total.shape[1])
            part.keep = jnp.where(s == 0, half_rows[0], half_rows[1])
            part.got = swap(jnp.where(s == 0, half_rows[1], half_rows[0]))
        for weight, pieces in WEIGHTS.items():
            names, places = places_of(weight, pieces)
            keep, got = (
                jnp.concatenate([getattr(sums[names[p]], k)[:, c : c + 128] for p, c in places], axis=1)
                for k in ("keep", "got")
            )
            flats[weight] = jnp.concatenate(interleave(keep, got, s, pieces), axis=1).reshape(-1)
        vec = lax.psum(made["table"], ("dp", "seq"))
        base = ff // width
        vectors = [vec[0:2]] + [vec[2 + base + i] for i in (2, 0, 1)] + [vec[2 : 2 + base].reshape(-1)]
        vectors += [vec[2 + base + i] for i in (5, 3, 4)]
    return (
        made["output"].reshape(row_count, half, width),
        made["pooled"][None],
        made["d_input"].reshape(row_count, half, width),
        *(flats[n] for n in ("qkv", "o", "in", "out")),
        *vectors,
    )


def as_bits(*orders):
    bits = {"x": 0, "y": 1, "1": 2, "2": 3}
    return tuple(tuple(bits[c] for c in order) for order in orders)


def solution(mesh):
    count = mesh.shape["dp"]
    in_specs = (P("dp", "seq", None),) + (P(),) * 12 + (P("dp", None), P("dp", "seq", None))
    out_specs = (
        P("dp", "seq", None),
        P("dp", None, None),
        P("dp", "seq", None),
    ) + (P(("dp", "seq")),) * 4 + (P(),) * 8
    return jax.shard_map(
        functools.partial(on_device, count == GROUPS, count),
        mesh=mesh, in_specs=in_specs, out_specs=out_specs, check_vma=False,
    )
```

```python
import functools
import math

import jax
import jax.numpy as jnp
from jax import lax
from jax.experimental import pallas as pl
from jax.experimental.pallas import tpu as pltpu
from jax.sharding import PartitionSpec as P

HEADS = 12
EPSILON = 1e-12
HIDE = -1e30
GROUPS = 16
BF = jnp.bfloat16
F32 = jnp.float32
MIB = 2**20
PIECES = 1
MERGE_US = 1.0
KERNEL_US = 1.0
WEIGHTS = {"out": 1, "in": 1, "qkv": 3, "o": 1}
PARTS = {
    "a": ("out", 0, 384, "y1x2", "12yx"),
    "b": ("in", 0, 1024, "y1x2", "xy12"),
    "c": ("in", 1024, 1536, "1yx2", "yx21"),
    "d": ("qkv", 0, 1152, "x2y1", "xy12"),
}
WITH_O = "c"
WITH_VECTORS = "d"
PLAN = (
    "BWD", "OUT", "BACK", "QKV", "IN", "INPUT", "out", "qkv", "in", "input", "out", "qkv",
    "in", "out", "qkv", "in", "out", "qkv", "in",
)


def sds(shape, dtype):
    return jax.ShapeDtypeStruct(shape, dtype)


def nn(left, right):
    return jnp.dot(left, right, preferred_element_type=F32)


def nt(left, right):
    return lax.dot_general(left, right, (((1,), (1,)), ((), ())), preferred_element_type=F32)


def tn(left, right):
    return lax.dot_general(left, right, (((0,), (0,)), ((), ())), preferred_element_type=F32)


class Line:
    def __init__(self):
        self.last = None

    def call(self, kernel, outs, *args, scratch=(), hbm=(), smem=(), name=None, vmem=16, us=KERNEL_US, end=False):
        if end:
            outs = [sds((8, 128), F32), *outs]
        specs = []
        lead = len(args)
        for i in range(lead):
            space = pltpu.HBM if i in hbm else pltpu.SMEM if i in smem else pltpu.VMEM
            specs.append(pl.BlockSpec(memory_space=space))
        args = [
            pltpu.with_memory_space_constraint(arg, pltpu.HBM) if i in hbm else arg
            for i, arg in enumerate(args)
        ]
        after = () if self.last is None else (self.last,)
        specs += [pl.BlockSpec(memory_space=pl.ANY) for _ in after]

        def body(*refs):
            rest = refs[lead + len(after) :]
            if end:
                rest[0][...] = jnp.zeros((8, 128), F32)
                rest = rest[1:]
            kernel(*refs[:lead], *rest)

        made = pl.pallas_call(
            body,
            out_shape=list(outs),
            in_specs=specs,
            out_specs=[pl.BlockSpec(memory_space=pltpu.VMEM) for _ in outs],
            scratch_shapes=list(scratch),
            compiler_params=pltpu.CompilerParams(vmem_limit_bytes=vmem * MIB),
            cost_estimate=pl.CostEstimate(flops=int(us * 1.1e9), bytes_accessed=1024, transcendentals=0),
            name=name,
        )(*args, *after)
        self.last = made[0]
        return made[1:] if end else made


def segment_of(positions, lens_ref):
    ids = jnp.zeros_like(positions)
    end = jnp.int32(0)
    for j in range(lens_ref.shape[1]):
        end = end + lens_ref[0, j]
        ids = ids + (positions >= end).astype(jnp.int32)
    return ids


def own_first(index, half, s):
    return jnp.where(index < half, index + s * half, index - half + (1 - s) * half)


def normalise(total):
    centered = total - jnp.mean(total, axis=-1, keepdims=True)
    inverse = lax.rsqrt(jnp.mean(centered * centered, axis=-1, keepdims=True) + EPSILON)
    return centered * inverse, inverse


def norm_pull(grad, normal, inverse, gain):
    scaled = grad * gain
    return inverse * (
        scaled
        - jnp.mean(scaled, axis=-1, keepdims=True)
        - normal * jnp.mean(scaled * normal, axis=-1, keepdims=True)
    )


def column_sum(matrix):
    return jnp.sum(matrix, axis=0, keepdims=True)


def copies_of(source, target, sems, first, pieces):
    rows = target.shape[0] // pieces
    return [
        pltpu.make_async_copy(
            source.at[i * rows : (i + 1) * rows, :], target.at[i * rows : (i + 1) * rows, :], sems.at[first + i]
        )
        for i in range(pieces)
    ]


def project_kernel(own_hbm, w_hbm, b_hbm, own, w_mine, bias, lin, b_buf, sems):
    width = own.shape[1]
    mine = width // 2
    s = lax.axis_index("seq")
    first = pltpu.make_async_copy(own_hbm, own, sems.at[3 * PIECES])
    first.start()
    copies = []
    for c in range(3):
        start = pl.multiple_of(c * width + s * mine, 128)
        copies.append(copies_of(w_hbm.at[:, pl.ds(start, mine)], w_mine.at[c], sems, c * PIECES, PIECES))
        for copy in copies[-1]:
            copy.start()
    second = pltpu.make_async_copy(b_hbm, b_buf, sems.at[3 * PIECES + 1])
    second.start()
    second.wait()
    column = pl.ds(pl.multiple_of(s * mine, 128), mine)
    bias[...] = jnp.zeros_like(bias)
    bias[0:1, :] = b_buf[0:1, column].astype(F32)
    bias[2:3, :] = b_buf[1:2, column].astype(F32)
    first.wait()
    for c in range(3):
        for copy in copies[c]:
            copy.wait()
        lin[:, c * mine : (c + 1) * mine] = nn(own[...], w_mine[c]) + bias[c : c + 1, :]


def attend_kernel(
    lens, other, w_mine, bias, lin, w_o_hbm, w_in_hbm, w_out_hbm,
    q_out, k_out, v_out, kt_out, expo_out, scale_out, att_t, att_out, w_o, w_in, w_out, sems,
):
    half, width = other.shape
    length = 2 * half
    mine = width // 2
    pair = 2 * (width // HEADS)
    head = pair // 2
    s = lax.axis_index("seq")
    copies = []
    for source, target in ((w_o_hbm, w_o), (w_in_hbm, w_in), (w_out_hbm, w_out)):
        copies += copies_of(source, target, sems, len(copies), PIECES)
    for copy in copies:
        copy.start()
    parts = []
    for c in range(3):
        rest = nn(other[...], w_mine[c]) + bias[c : c + 1, :]
        parts.append(jnp.concatenate([lin[:, c * mine : (c + 1) * mine], rest], axis=0))
    q_all, k_all, v_all = parts
    q_all = q_all.astype(BF).astype(F32) * (1.0 / math.sqrt(head))
    q_out[...] = q_all.astype(BF)
    k_out[...] = k_all.astype(BF)
    v_out[...] = v_all.astype(BF)
    kt_out[...] = k_all.T.astype(BF)
    vt = v_all.T.astype(BF)
    rows = own_first(lax.broadcasted_iota(jnp.int32, (length, pair), 0), half, s)
    lane = lax.broadcasted_iota(jnp.int32, (length, pair), 1)
    same = segment_of(rows, lens) == lane % head
    in_range = lane % head < lens.shape[1]
    mark_k = jnp.where(same, 1.0, 0.0)
    mark_q = jnp.where(jnp.logical_and(in_range, jnp.logical_not(same)), HIDE, 0.0)
    first = lane < head
    for j in range(mine // pair):
        cols = slice(j * pair, (j + 1) * pair)
        q2, k2 = q_all[:, cols], k_all[:, cols]
        pieces = []
        for a in range(2):
            keep = first if a == 0 else jnp.logical_not(first)
            k_m = jnp.where(keep, k2, mark_k).astype(BF)
            q_m = jnp.where(keep, q2, mark_q).astype(BF)
            scores = nt(k_m, q_m)
            top = jnp.max(scores, axis=0, keepdims=True)
            expo = jnp.exp(scores - top)
            scale = 1.0 / jnp.sum(expo, axis=0, keepdims=True)
            low = expo.astype(BF)
            h = 2 * j + a
            expo_out[h] = low
            scale_out[h : h + 1, :] = scale
            pieces.append(nn(vt[h * head : (h + 1) * head, :], low) * scale)
        both = jnp.concatenate(pieces, axis=0)
        att_t[cols, :] = both
        att_out[:, cols] = both.T.astype(BF)
    for copy in copies:
        copy.wait()


def forward_kernel(
    lens,
    own,
    att_mine,
    att_got,
    w_o,
    b_o,
    gain1,
    shift1,
    w_in,
    b_in,
    w_out,
    b_out,
    gain2,
    shift2,
    cot,
    mid_out,
    active_out,
    pull_out,
    normal_out,
    inverse_out,
    sum2_out,
    down_keep,
    down_send,
    out_out,
    pool_out,
    vec_out,
    down_acc,
):
    half, width = own.shape
    mine = width // 2
    ff = w_in.shape[1]
    s = lax.axis_index("seq")
    row_a = pl.ds(pl.multiple_of(s * mine, 128), mine)
    row_b = pl.ds(pl.multiple_of((1 - s) * mine, 128), mine)
    branch = nn(att_mine[0:half, :], w_o[row_a, :]) + nn(att_got[half:, :], w_o[row_b, :])
    normal, inverse = normalise(own[...].astype(F32) + (branch + b_o[...].astype(F32)))
    middle = normal * gain1[...].astype(F32) + shift1[...].astype(F32)
    low = middle.astype(BF)
    mid_out[...] = low
    normal_out[...] = normal
    inverse_out[...] = inverse
    down_acc[...] = middle + b_out[...].astype(F32)
    step = 1536
    for c in range(0, ff, step):
        cols = slice(c, c + step)
        upper = nn(low, w_in[:, cols]) + b_in[:, cols].astype(F32)
        cdf = 0.5 + 0.5 * lax.erf(upper * (1.0 / math.sqrt(2.0)))
        density = jnp.exp(-0.5 * upper * upper) * (1.0 / math.sqrt(2.0 * math.pi))
        act = (upper * cdf).astype(BF)
        active_out[:, cols] = act
        pull_out[:, cols] = cdf + upper * density
        down_acc[...] += nn(act, w_out[cols, :])
    normal2, inverse2 = normalise(down_acc[...])
    gain = gain2[...].astype(F32)
    final = normal2 * gain + shift2[...].astype(F32)
    out_out[...] = final.astype(BF)
    rows = lax.broadcasted_iota(jnp.int32, (half, 1), 0) + s * half
    ids = segment_of(rows, lens)
    pool_out[...] = jnp.zeros_like(pool_out)
    for t in range(lens.shape[1]):
        pool_out[t : t + 1, :] = column_sum(jnp.where(ids == t, final, 0.0))
    grad = cot[...].astype(F32)
    sum2 = norm_pull(grad, normal2, inverse2, gain)
    sum2_out[...] = sum2
    down = sum2.astype(BF)
    down_acc[...] = sum2
    down_keep[...] = down_acc[:, row_a].astype(BF)
    down_send[...] = down_acc[:, row_b].astype(BF)
    vec_out[...] = jnp.zeros_like(vec_out)
    vec_out[0:1, :] = column_sum(grad * normal2)
    vec_out[1:2, :] = column_sum(grad)
    vec_out[2:3, :] = column_sum(down.astype(F32))


def backward_kernel(
    sum2, pull, normal, inverse, gain1, w_in, w_out,
    up_keep, up_send, sum1_out, branch_out, vec_out, mid_acc,
):
    width, ff = w_in.shape
    s = lax.axis_index("seq")
    step = 768
    per = ff // 2 // step
    mid_acc[...] = sum2[...]
    low = sum2[...].astype(BF)
    vec_out[...] = jnp.zeros_like(vec_out)
    sums = []
    for i in range(2 * per):
        block = (i // per + s) % 2
        start = pl.multiple_of(block * (ff // 2) + (i % per) * step, 128)
        cols = pl.ds(start, step)
        grad_upper = (nt(low, w_out[cols, :]) * pull[:, cols]).astype(BF)
        place = up_keep if i < per else up_send
        place[:, (i % per) * step : (i % per + 1) * step] = grad_upper
        sums.append(column_sum(grad_upper.astype(F32)))
        mid_acc[...] += nt(grad_upper, w_in[:, cols])
    ups = [jnp.concatenate(sums[:per], axis=1), jnp.concatenate(sums[per:], axis=1)]
    for b in range(2):
        line = jnp.where(s == b, ups[0], ups[1])
        for r in range(ff // 2 // width):
            row = b * (ff // 2 // width) + r
            vec_out[row : row + 1, :] = line[:, r * width : (r + 1) * width]
    base = ff // width
    grad_mid = mid_acc[...]
    vec_out[base : base + 1, :] = column_sum(grad_mid * normal[...])
    vec_out[base + 1 : base + 2, :] = column_sum(grad_mid)
    sum1 = norm_pull(grad_mid, normal[...], inverse[...], gain1[...].astype(F32))
    sum1_out[...] = sum1
    branch = sum1.astype(BF)
    branch_out[...] = branch
    vec_out[base + 2 : base + 3, :] = column_sum(branch.astype(F32))


def attend_back_kernel(
    branch_own, branch_got, w_o, q, k, v, kt, expo, scale, att_t, grad_out, vec_out
):
    length, mine = q.shape
    width = w_o.shape[1]
    head = width // HEADS
    pair = 2 * head
    s = lax.axis_index("seq")
    w_mine = w_o[pl.ds(pl.multiple_of(s * mine, 128), mine), :]
    grad_t = jnp.concatenate([nt(w_mine, branch_own[...]), nt(w_mine, branch_got[...])], axis=1)
    lane = lax.broadcasted_iota(jnp.int32, (length, pair), 1)
    first = lane < head
    vec_out[...] = jnp.zeros_like(vec_out)
    for j in range(mine // pair):
        cols = slice(j * pair, (j + 1) * pair)
        q2 = q[:, cols]
        v2 = v[:, cols].astype(F32)
        scaled, inners = [], []
        for h in (2 * j, 2 * j + 1):
            part = slice(h * head, (h + 1) * head)
            times = scale[h : h + 1, :]
            scaled.append(grad_t[part, :] * times)
            inners.append(jnp.sum(att_t[part, :] * scaled[-1], axis=0, keepdims=True))
        a2 = jnp.concatenate(scaled, axis=0).astype(BF)
        dq, dk, dv = [], [], []
        for a in range(2):
            h = 2 * j + a
            keep = first if a == 0 else jnp.logical_not(first)
            v_m = jnp.where(keep, v2, 0.0).astype(BF)
            grad_p = nn(v_m, a2)
            low = expo[h]
            raw = (low.astype(F32) * (grad_p - inners[a])).astype(BF)
            dk.append(nn(raw, q2))
            dv.append(nt(low, a2))
            dq.append(nn(kt[h * head : (h + 1) * head, :], raw))
        dq_low = (jnp.concatenate(dq, axis=0) * (1.0 / math.sqrt(head))).astype(BF).T
        dk_low = jnp.where(first, dk[0], dk[1]).astype(BF)
        dv_low = jnp.where(first, dv[0], dv[1]).astype(BF)
        grad_out[:, cols] = dq_low
        grad_out[:, mine + j * pair : mine + (j + 1) * pair] = dk_low
        grad_out[:, 2 * mine + j * pair : 2 * mine + (j + 1) * pair] = dv_low
        vec_out[0:1, cols] = column_sum(dq_low.astype(F32))
        vec_out[1:2, cols] = column_sum(dv_low.astype(F32))


def chunk_of(slot, order):
    if order is None:
        return slot
    chunks = []
    for bits in order:
        rel = 0
        for i, bit in enumerate(bits):
            rel |= (slot >> (len(bits) - 1 - i) & 1) << bit
        chunks.append(rel)
    rel = jnp.where(lax.axis_index("seq") == 0, jnp.int32(chunks[0]), jnp.int32(chunks[1]))
    return jnp.bitwise_xor(rel, lax.axis_index("dp"))


def spread_rows(whole, order, keep, send, cols, to):
    rows = whole.shape[0] // GROUPS
    for slot in range(GROUPS):
        chunk = chunk_of(slot, order)
        target = keep if slot < GROUPS // 2 else send
        place = slot % (GROUPS // 2) * rows
        target[place : place + rows, to] = whole[pl.ds(pl.multiple_of(chunk * rows, 16), rows), cols]


def grad_out_kernel(parts, active_own, active_got, down_own, down_got, *outs):
    *outs, whole = outs
    block = 512
    for i in range(0, active_own.shape[1], block):
        cols = slice(i, i + block)
        whole[cols, :] = (
            tn(active_own[:, cols], down_own[...]) + tn(active_got[:, cols], down_got[...])
        ).astype(BF)
    for p, (start, stop, order) in enumerate(parts):
        spread_rows(whole, order, outs[2 * p], outs[2 * p + 1], slice(start, stop), slice(0, stop - start))


def grad_in_kernel(
    parts, with_o, mid_own, mid_got, up_own, up_got, att_mine, att_got, branch_own, branch_got, *outs
):
    *outs, whole, whole_o = outs
    half, width = mid_own.shape
    mine = width // 2
    for i in range(2):
        cols = slice(i * mine, (i + 1) * mine)
        own_t, got_t = mid_own[:, cols].T, mid_got[:, cols].T
        for n in range(0, up_own.shape[1], 512):
            out = slice(n, n + 512)
            whole[cols, out] = (nn(own_t, up_own[:, out]) + nn(got_t, up_got[:, out])).astype(BF)
    s = lax.axis_index("seq")
    column = pl.ds(pl.multiple_of(s * mine, 128), mine)
    mine_o = tn(att_mine[0:half, :], branch_own[:, column]) + tn(att_mine[half:, :], branch_got[:, column])
    got_o = tn(att_got[half:, :], branch_own[:, column]) + tn(att_got[0:half, :], branch_got[:, column])
    for i in range(2):
        whole_o[i * mine : (i + 1) * mine, :] = jnp.where(s == i, mine_o, got_o).astype(BF)
    for p, (start, stop, order) in enumerate(parts):
        spread_rows(whole, order, outs[2 * p], outs[2 * p + 1], slice(start, stop), slice(0, stop - start))
        if p == with_o:
            to = slice(stop - start, stop - start + mine)
            spread_rows(whole_o, order, outs[2 * p], outs[2 * p + 1], slice(0, mine), to)


USED = 12


def pack_vectors(table, send, start):
    total = table.shape[1]
    high = table.astype(BF).astype(F32)
    rest = (table - high).astype(BF).astype(F32)
    half = total // 2
    if send.shape[1] >= total + half:
        more = jnp.concatenate([rest[4:8, half:], rest[8:USED, half:]], axis=1)
        send[start : start + 16, 0:total] = jnp.concatenate([high[0:USED, :], more], axis=0).astype(BF)
        side = jnp.concatenate([rest[0:USED, 0:half], rest[0:4, half:]], axis=0)
        send[start : start + 16, total : total + half] = side.astype(BF)
    else:
        width = min(total, send.shape[1])
        row = start
        for piece in (high, rest):
            for c in range(0, total, width):
                send[row : row + 16, 0:width] = piece[:, c : c + width].astype(BF)
                row += 16
    return high + rest


def unpack_vectors(got, start, total):
    half = total // 2
    if got.shape[1] >= total + half:
        first = got[start : start + 16, 0:total].astype(F32)
        side = got[start : start + 16, total : total + half].astype(F32)
        right = jnp.concatenate([side[USED:, :], first[USED:, 0:half], first[USED:, half:]], axis=0)
        rest = jnp.concatenate([side[0:USED, :], right], axis=1)
        return jnp.concatenate([first[0:USED, :] + rest, jnp.zeros((16 - USED, total), F32)], axis=0)
    width = min(total, got.shape[1])
    count = total // width
    parts = [got[start + 16 * i : start + 16 * (i + 1), 0:width].astype(F32) for i in range(2 * count)]
    return jnp.concatenate([parts[i] + parts[count + i] for i in range(count)], axis=1)


def vector_rows(total, cols, whole=False):
    pieces = total // min(total, cols)
    return 16 * pieces * (1 if whole or cols >= total + total // 2 else 2)


def grad_qkv_kernel(parts, with_vectors, own, other, grads, vec_f, vec_b, vec_a, *outs):
    *outs, whole = outs
    half, width = own.shape
    mine = width // 2
    rows = width // GROUPS
    s = lax.axis_index("seq")
    for i in range(2):
        cols = slice(i * mine, (i + 1) * mine)
        both_t = jnp.concatenate([own[:, cols].T, other[:, cols].T], axis=1)
        for c in range(3):
            out = slice(c * mine, (c + 1) * mine)
            whole[cols, out] = nn(both_t, grads[:, out]).astype(BF)
    for p, (start, stop, order) in enumerate(parts):
        spread_rows(whole, order, outs[2 * p], outs[2 * p + 1], slice(start, stop), slice(0, stop - start))
    zero = jnp.zeros((1, mine), F32)
    lines = []
    for r in range(2):
        line = vec_a[r : r + 1, :]
        lines.append(
            jnp.concatenate([jnp.where(s == 0, line, zero), jnp.where(s == 0, zero, line)], axis=1)
        )
    table = jnp.concatenate(lines + [vec_b[0:7, :], vec_f[0:3, :], jnp.zeros((4, width), F32)], axis=0)
    outs[-1][...] = pack_vectors(table, outs[2 * with_vectors + 1], GROUPS // 2 * rows)


def grad_input_kernel(grads, w_mine, sum1, pool, keep, send):
    half, width = sum1.shape
    mine = width // 2
    a, b = sum1[...], jnp.zeros((half, width), F32)
    for c in range(3):
        cols = slice(c * mine, (c + 1) * mine)
        a = a + nt(grads[0:half, cols], w_mine[c])
        b = b + nt(grads[half:, cols], w_mine[c])
    keep[...] = a
    send[0:half, :] = b
    send[half:, :] = pool[...]


def merge_kernel(rows, got, keep, keep_out, send_out):
    total = keep[0:rows, :].astype(F32) + got[0:rows, :].astype(F32)
    keep_out[...] = total[0 : rows // 2, :].astype(BF)
    send_out[...] = total[rows // 2 :, :].astype(BF)


def merge_vec_kernel(rows, got, keep, vec, keep_out, send_out, vec_out):
    merge_kernel(rows, got, keep, keep_out, send_out.at[0 : rows // 2, :])
    table = vec[...] + unpack_vectors(got, rows, vec.shape[1])
    vec_out[...] = pack_vectors(table, send_out, rows // 2)


def last_kernel(got, keep, keep_out, send_out, acc):
    rows = keep.shape[0]
    s = lax.axis_index("seq")
    acc[...] = keep[...].astype(F32) + got[0:rows, :].astype(F32)
    keep_out[...] = acc[pl.ds(pl.multiple_of(s * (rows // 2), 8), rows // 2), :]
    send_out[...] = acc[pl.ds(pl.multiple_of((1 - s) * (rows // 2), 8), rows // 2), :]


def last_vec_kernel(got, keep, vec, keep_out, send_out, acc):
    rows = keep.shape[0]
    last_kernel(got, keep, keep_out, send_out.at[0 : rows // 2, :], acc)
    table = vec[...] + unpack_vectors(got, rows, vec.shape[1])
    width = min(table.shape[1], keep.shape[1])
    for i, c in enumerate(range(0, table.shape[1], width)):
        send_out[rows // 2 + 16 * i : rows // 2 + 16 * (i + 1), 0:width] = table[:, c : c + width]


def finish_kernel(pieces, places, *refs):
    flat = refs[-1]
    count = len(places)
    per = count // pieces
    s = lax.axis_index("seq")
    for j, (p, lane) in enumerate(places):
        keep, got = refs[2 * p], refs[2 * p + 1]
        rows = keep.shape[0]
        cols = slice(lane, lane + 128)
        first, second = keep[:, cols], got[0:rows, cols]
        line = j // per * 2 * per + j % per
        flat[pl.ds(line, rows, stride=2 * count), :] = jnp.where(s == 0, first, second)
        flat[pl.ds(line + per, rows, stride=2 * count), :] = jnp.where(s == 0, second, first)


def finish_vectors_kernel(rows, width, sent, got, b_qv, b_o, gain1, shift1, b_in, b_out, gain2, shift2):
    half = min(width, sent.shape[1])
    count = width // half
    total = sent[rows:, 0:half] + got[rows:, 0:half]
    table = jnp.concatenate([total[16 * i : 16 * (i + 1), :] for i in range(count)], axis=1)
    b_qv[...] = table[0:2, :]
    base = b_in.shape[0] * 128 // width
    for r in range(base):
        for c in range(width // 128):
            line = r * (width // 128) + c
            b_in[line : line + 1, :] = table[2 + r : 3 + r, c * 128 : (c + 1) * 128]
    for i, ref in enumerate((gain1, shift1, b_o, gain2, shift2, b_out)):
        for c in range(width // 128):
            ref[c : c + 1, :] = table[2 + base + i : 3 + base + i, c * 128 : (c + 1) * 128]


def finish_input_kernel(lens, keep, sent, got, final, d_input, pooled, output):
    half = keep.shape[0]
    output[...] = final[...]
    d_input[...] = keep[...] + got[0:half, :]
    total = sent[half:, :] + got[half:, :]
    for t in range(lens.shape[1]):
        pooled[t : t + 1, :] = total[t : t + 1, :] / lens[0, t].astype(F32)


def swap(x, axis="seq"):
    return lax.ppermute(x, axis, [(0, 1), (1, 0)])


def send_to(x, phase, order, count):
    pairs = []
    for d in range(count):
        for s in range(2):
            pairs.append((2 * d + s, 2 * (d ^ (1 << order[s][phase])) + s))
    return lax.ppermute(x, ("dp", "seq"), pairs)


class Part:
    def __init__(self, keep, send, order, vec):
        self.keep, self.sent, self.order, self.vec, self.got = keep, send, order, vec, None


class Sum:
    def __init__(self, line, parts, count, name):
        self.line, self.parts, self.count, self.name = line, parts, count, name
        self.phase = 0
        self.send()

    def send(self):
        for part in self.parts:
            if self.phase == len(part.order[0]):
                part.got = swap(part.sent)
            else:
                part.got = send_to(part.sent, self.phase, part.order, self.count)

    def step(self):
        last = self.phase == len(self.parts[0].order[0]) - 1
        dtype = F32 if last else BF
        args, outs, scratch, jobs = [], [], [], []
        for part in self.parts:
            rows, cols = part.keep.shape
            half = rows // 2
            extra = 0 if part.vec is None else vector_rows(part.vec.shape[1], cols, last)
            args += [part.got, part.keep]
            outs += [sds((half, cols), dtype), sds((half + extra, cols), dtype)]
            if last:
                scratch.append(pltpu.VMEM((rows, cols), F32))
            if part.vec is None:
                jobs.append((last_kernel if last else functools.partial(merge_kernel, rows), 2, 2))
            elif last:
                args.append(part.vec)
                jobs.append((last_vec_kernel, 3, 2))
            else:
                args.append(part.vec)
                outs.append(sds(part.vec.shape, F32))
                jobs.append((functools.partial(merge_vec_kernel, rows), 3, 3))

        def kernel(*refs):
            i, o, t = 0, len(args), len(args) + len(outs)
            for run, reads, writes in jobs:
                run(*refs[i : i + reads], *refs[o : o + writes], *([refs[t]] if last else []))
                i, o, t = i + reads, o + writes, t + 1

        made = self.line.call(
            kernel, outs, *args, scratch=scratch, name=f"sum_{self.name}_{self.phase}", vmem=10, us=MERGE_US
        )
        made = list(made)
        for part, (_, _, writes) in zip(self.parts, jobs):
            part.keep, part.sent = made[0], made[1]
            if writes == 3:
                part.vec = made[2]
            del made[:writes]
        self.phase += 1
        self.send()


def interleave(keep, got, s, pieces):
    size = keep.shape[1] // pieces
    outs = []
    for i in range(pieces):
        a, b = keep[:, i * size : (i + 1) * size], got[:, i * size : (i + 1) * size]
        outs += [jnp.where(s == 0, a, b), jnp.where(s == 0, b, a)]
    return outs


def on_device(
    spread, count,
    hidden_in, w_qkv, b_qv, w_o, b_o, ln1_gain, ln1_bias, w_in, b_in, w_out, b_out, ln2_gain, ln2_bias,
    seg_lengths, cotangent,
):
    row_count, half, width = hidden_in.shape
    length = 2 * half
    mine = width // 2
    heads = HEADS // 2
    ff = w_in.shape[1]
    s = lax.axis_index("seq")
    own = hidden_in.reshape(half, width)
    cot = cotangent.reshape(half, width)
    line = Line()
    call = line.call
    flat = lambda x: x.reshape(1, -1)
    rows_ff, rows_w = ff // GROUPS, width // GROUPS
    half_ff, half_w = GROUPS // 2 * rows_ff, GROUPS // 2 * rows_w
    made, sums, flats = {}, {}, {}

    def parts_of(weight):
        names = [n for n in PARTS if PARTS[n][0] == weight]
        return names, tuple(
            (PARTS[n][1], PARTS[n][2], as_bits(*PARTS[n][3:]) if spread else None) for n in names
        )

    def reduce(names, arrays):
        for i, name in enumerate(names):
            keep, send = arrays[2 * i], arrays[2 * i + 1]
            vec = made["table"] if name == WITH_VECTORS else None
            sums[name] = Part(keep, send, as_bits(*PARTS[name][3:]), vec)
        if spread:
            weight = PARTS[names[0]][0]
            sums[weight] = Sum(line, [sums[n] for n in names], count, weight)

    other = swap(own)
    own, w_mine, bias, lin = call(
        project_kernel,
        [sds((half, width), BF), sds((3, width, mine), BF), sds((8, mine), F32), sds((half, 3 * mine), F32)],
        own, w_qkv, b_qv,
        hbm=(0, 1, 2), scratch=[pltpu.VMEM(b_qv.shape, BF), pltpu.SemaphoreType.DMA((3 * PIECES + 2,))],
        name="project", vmem=12,
    )
    q, k, v, kt, expo, scale, att_t, att_mine, w_o, w_in, w_out = call(
        attend_kernel,
        [sds((length, mine), BF)] * 3
        + [sds((mine, length), BF), sds((heads, length, length), BF), sds((8, length), F32)]
        + [sds((mine, length), F32), sds((length, mine), BF)]
        + [sds(w.shape, BF) for w in (w_o, w_in, w_out)],
        seg_lengths, other, w_mine, bias, lin, w_o, w_in, w_out,
        smem=(0,), hbm=(5, 6, 7), scratch=[pltpu.SemaphoreType.DMA((3 * PIECES,))], name="attend", vmem=16,
    )
    att_got = swap(att_mine)
    (mid_low, active, pull, normal, inverse, sum2, down_own, down_send, output, pool_part, vec_f) = call(
        forward_kernel,
        [
            sds((half, width), BF), sds((half, ff), BF), sds((half, ff), F32), sds((half, width), F32),
            sds((half, 1), F32), sds((half, width), F32), sds((half, mine), BF), sds((half, mine), BF),
            sds((half, width), BF), sds((8, width), F32), sds((8, width), F32),
        ],
        seg_lengths, own, att_mine, att_got, w_o, flat(b_o), flat(ln1_gain), flat(ln1_bias), w_in, flat(b_in),
        w_out, flat(b_out), flat(ln2_gain), flat(ln2_bias), cot,
        smem=(0,), scratch=[pltpu.VMEM((half, width), F32)], name="forward", vmem=16,
    )
    active_got = swap(active)
    mid_got = swap(mid_low)
    down_got = swap(down_send)

    def backward():
        made["up_own"], up_send, made["sum1"], branch, made["vec_b"] = call(
            backward_kernel,
            [
                sds((half, ff // 2), BF), sds((half, ff // 2), BF), sds((half, width), F32),
                sds((half, width), BF), sds((8, width), F32),
            ],
            sum2, pull, normal, inverse, flat(ln1_gain), w_in, w_out,
            scratch=[pltpu.VMEM((half, width), F32)], name="backward", vmem=12,
        )
        made["branch"] = branch, swap(branch)
        made["up_got"] = swap(up_send)

    def grad_out():
        names, parts = parts_of("out")
        outs = [sds((half_ff, stop - start), BF) for start, stop, _ in parts for _ in range(2)]
        arrays = call(
            functools.partial(grad_out_kernel, parts), outs,
            active, active_got, down_own, down_got, name="grad_out",
            scratch=[pltpu.VMEM((ff, mine), BF)],
        )
        reduce(names, arrays)

    def grad_in():
        names, parts = parts_of("in")
        with_o = names.index(WITH_O)
        outs = []
        for i, (start, stop, _) in enumerate(parts):
            outs += [sds((half_w, stop - start + (mine if i == with_o else 0)), BF)] * 2
        arrays = call(
            functools.partial(grad_in_kernel, parts, with_o), outs,
            mid_low, mid_got, made["up_own"], made["up_got"], att_mine, att_got, *made["branch"], name="grad_in",
            scratch=[pltpu.VMEM((width, ff // 2), BF), pltpu.VMEM((width, mine), BF)],
        )
        reduce(names, arrays)

    def attend_back():
        made["grads"], made["vec_a"] = call(
            attend_back_kernel, [sds((length, 3 * mine), BF), sds((8, mine), F32)],
            *made["branch"], w_o, q, k, v, kt, expo, scale, att_t, name="attend_back", vmem=16,
        )

    def grad_qkv():
        names, parts = parts_of("qkv")
        with_vectors = names.index(WITH_VECTORS)
        outs = []
        for i, (start, stop, _) in enumerate(parts):
            extra = vector_rows(width, stop - start) if i == with_vectors else 0
            outs += [sds((half_w, stop - start), BF), sds((half_w + extra, stop - start), BF)]
        outs.append(sds((16, width), F32))
        *arrays, made["table"] = call(
            functools.partial(grad_qkv_kernel, parts, with_vectors), outs,
            own, other, made["grads"], vec_f, made["vec_b"], made["vec_a"], name="grad_qkv",
            scratch=[pltpu.VMEM((width, 3 * mine), BF)],
        )
        reduce(names, arrays)

    def grad_input():
        made["keep"], made["send"] = call(
            grad_input_kernel, [sds((half, width), F32), sds((half + 8, width), F32)],
            made["grads"], w_mine, made["sum1"], pool_part, name="grad_input",
        )
        made["got"] = swap(made["send"])

    def finish_input():
        made["d_input"], made["pooled"], made["output"] = call(
            finish_input_kernel,
            [sds((half, width), F32), sds((seg_lengths.shape[1], width), F32), sds((half, width), BF)],
            seg_lengths, made["keep"], made["send"], made["got"], output, smem=(0,), name="finish_input", end=True,
        )

    def places_of(weight, pieces):
        if weight == "o":
            start, stop = PARTS[WITH_O][1:3]
            return [WITH_O], [(0, stop - start + c) for c in range(0, mine, 128)]
        names, parts = parts_of(weight)
        return names, [
            (i, c - start) for i, (start, stop, _) in enumerate(parts) for c in range(start, stop, 128)
        ]

    def finish_all():
        args, outs, jobs = [], [], []
        for weight, pieces in WEIGHTS.items():
            names, places = places_of(weight, pieces)
            first = len(args)
            args += [x for n in names for x in (sums[n].keep, sums[n].got)]
            outs.append(sds((2 * args[first].shape[0] * len(places), 128), F32))
            jobs.append((functools.partial(finish_kernel, pieces, places), first, len(args)))
        part = sums[WITH_VECTORS]
        one = sds((width // 128, 128), F32)
        args += [part.sent, part.got]
        outs += [sds((2, width), F32), one, one, one, sds((ff // 128, 128), F32), one, one, one]

        def kernel(*refs):
            results = refs[len(args) :]
            sent, got = refs[len(args) - 2 : len(args)]
            for job, (run, start, stop) in enumerate(jobs):
                run(*refs[start:stop], results[job])
            finish_vectors_kernel(part.keep.shape[0], width, sent, got, *results[len(jobs) :])

        done = call(kernel, outs, *args, name="finish", vmem=10)
        for weight, out in zip(WEIGHTS, done):
            flats[weight] = out.reshape(-1)
        made["vectors"] = done[len(jobs) :]

    work = {
        "BWD": backward, "OUT": grad_out, "IN": grad_in, "BACK": attend_back, "QKV": grad_qkv, "INPUT": grad_input,
        "input": finish_input,
    }
    for item in PLAN:
        if item in work:
            work[item]()
        elif spread:
            sums[item].step()
    if spread:
        finish_all()

    if spread:
        vectors = [v if v.shape[0] == 2 else v.reshape(-1) for v in made["vectors"]]
    else:
        for name in PARTS:
            part = sums[name]
            both = jnp.concatenate([part.keep, part.sent[: part.keep.shape[0]]], axis=0)
            total = lax.psum_scatter(both, "dp", scatter_dimension=0, tiled=True).astype(F32)
            half_rows = total.reshape(2, -1, total.shape[1])
            part.keep = jnp.where(s == 0, half_rows[0], half_rows[1])
            part.got = swap(jnp.where(s == 0, half_rows[1], half_rows[0]))
        for weight, pieces in WEIGHTS.items():
            names, places = places_of(weight, pieces)
            keep, got = (
                jnp.concatenate([getattr(sums[names[p]], k)[:, c : c + 128] for p, c in places], axis=1)
                for k in ("keep", "got")
            )
            flats[weight] = jnp.concatenate(interleave(keep, got, s, pieces), axis=1).reshape(-1)
        vec = lax.psum(made["table"], ("dp", "seq"))
        base = ff // width
        vectors = [vec[0:2]] + [vec[2 + base + i] for i in (2, 0, 1)] + [vec[2 : 2 + base].reshape(-1)]
        vectors += [vec[2 + base + i] for i in (5, 3, 4)]
    return (
        made["output"].reshape(row_count, half, width),
        made["pooled"][None],
        made["d_input"].reshape(row_count, half, width),
        *(flats[n] for n in ("qkv", "o", "in", "out")),
        *vectors,
    )


def as_bits(*orders):
    bits = {"x": 0, "y": 1, "1": 2, "2": 3}
    return tuple(tuple(bits[c] for c in order) for order in orders)


def solution(mesh):
    count = mesh.shape["dp"]
    in_specs = (P("dp", "seq", None),) + (P(),) * 12 + (P("dp", None), P("dp", "seq", None))
    out_specs = (
        P("dp", "seq", None),
        P("dp", None, None),
        P("dp", "seq", None),
    ) + (P(("dp", "seq")),) * 4 + (P(),) * 8
    return jax.shard_map(
        functools.partial(on_device, count == GROUPS, count),
        mesh=mesh, in_specs=in_specs, out_specs=out_specs, check_vma=False,
    )
```
